256 devices in a mesh: ep: 32 (over x_lo, z, core), tp: 8 (over x_hi, y).
Axes of the slice: x: 4 (x_hi: 2, x_lo: 2; x = x_hi * 2 + x_lo), y: 4, z: 8, core: 2. Of those that a mesh axis runs over, the one named last changes fastest.
Arguments:
- residual_in: bfloat16 [6144, 2048], P('ep'), may hold values from -6 to 6
- shortcut: bfloat16 [6144, 2048], P('ep'), may hold values from -6 to 6
- attn_gain: float32 [2048], replicated, may hold values from 0.25 to 1.75
- moe_gain: float32 [2048], replicated, may hold values from 0.25 to 1.75
- query_weight: bfloat16 [2048, 4096], P('ep', 'tp')
- key_value: bfloat16 [2048, 1024], P('ep')
- output_weight: bfloat16 [2048, 4096], P('ep', 'tp'), may hold values from -0.09375 to 0.09375
- query_gain: float32 [128], replicated, may hold values from 0.5 to 5
- key_gain: float32 [128], replicated, may hold values from 0.5 to 5
- router_weight: bfloat16 [128, 2048], replicated, may hold values from -0.125 to 0.125
- expert_ids: int32 [6144, 8], P('ep'), may hold values from 0 to 127, all different within a row; in each aligned block of 192 rows (0 to 191, 192 to 383, ...) at most 15 rows name the same one
- gate_up_weight: bfloat16 [256, 2048, 1536], P(('ep', 'tp')), may hold values from -0.125 to 0.125
- down_weight: bfloat16 [256, 768, 2048], P(('ep', 'tp')), may hold values from -0.15625 to 0.15625
Outputs:
- layer_out: bfloat16 [6144, 2048], P('ep')
The draws below stay inside these ranges and needn't reach their ends.
Inputs may be any that keep to these rules, and one draw needn't show every extreme that they name: `expert_ids`: each row names 8 different experts. Among the 192 rows of one sequence no expert is named by more than 15 rows, a bound that some block reaches.
All inputs are finite; a program needn't handle non-finite values.
Results may differ from the reference program's by a relative error of at most 0.009.
Values may be sent and summed in bfloat16 or wider, within the bound.
No kernel may reach another device: no remote copies, remote signals or barrier semaphores. Data moves between devices by JAX's collectives and lax.ppermute only.
A program may use at most 128 MiB of HBM per device.

```python
import math
import jax
import jax.numpy as jnp
import numpy as np
from jax import lax

D = 2048
HD = 128
QH = 32
KVH = 4
FF = 1536
TOPK = 8
ROWS = 192
EXPERTS = 128
TOKENS = 6144
QH_DEV = 4
GROUP = 8
FF_DEV = 768
CAP = 15
N_EP = 32
N_TP = 8


def common_base(key):
    return jax.random.normal(jax.random.fold_in(key, 97), (D, KVH * HD), jnp.float32)


def draw_query_weight(key, part):
    key = jax.random.fold_in(key, 11)
    noise = jax.random.normal(key, (D, QH * HD), jnp.float32)
    mixed = noise
    return (mixed * D ** (-0.5)).astype(jnp.bfloat16)


def draw_key_value(key, part):
    base = common_base(key)
    key = jax.random.fold_in(key, 23)
    values = jax.random.normal(key, (D, KVH * HD), jnp.float32)
    return (jnp.concatenate([base, values], 1) * D ** (-0.5)).astype(jnp.bfloat16)


def draw_query_gain(key, part):
    key = jax.random.fold_in(key, 31)
    return jax.random.uniform(key, (HD,), jnp.float32, 0.5, 1.5)


def draw_key_gain(key, part):
    key = jax.random.fold_in(key, 37)
    return jax.random.uniform(key, (HD,), jnp.float32, 0.5, 1.5)


def level_of(key, dims, split, least, top_value):
    level = 1.0
    for axis_at, blocks in split:
        steps = jax.random.uniform(jax.random.fold_in(jax.random.fold_in(key, 6), axis_at), (blocks,), jnp.float32, least / len(split), top_value / len(split))
        level = level * jnp.repeat(jnp.exp(steps), dims[axis_at] // blocks).reshape((-1,) + (1,) * (len(dims) - 1 - axis_at))
    return level


def routed_block(key, own, number, rows, amount, top, limit, skew):
    sequence = jax.random.permutation(key, amount)
    packed, usual = portions_of(amount, rows * top, limit, skew, True), portions_of(amount, rows * top, limit, skew, False)
    places = jnp.arange(amount)

    def named(lengths, rotation):
        used = int((lengths > 0).sum())
        fixed = max(1, used // 4)
        moved = fixed + (places - fixed + rotation * (used - fixed)) % max(1, amount - fixed)
        return jnp.zeros((amount,), jnp.int32).at[sequence[jnp.where(places < fixed, places, moved)]].set(jnp.asarray(lengths, jnp.int32))

    lengths = jnp.where(number % 4 == 0, named(packed, number // 4), named(usual, number - number // 4 - 1))
    mixed = jax.random.permutation(jax.random.fold_in(own, 3), amount)
    donor, receiver = mixed[0:amount // 2 * 2:2], mixed[1:amount // 2 * 2:2]
    margin = jnp.minimum(lengths[donor] - 1, limit - lengths[receiver]) // 2
    margin = jnp.where((donor == sequence[0]) | (receiver == sequence[0]) | (lengths[receiver] == 0), 0, jnp.maximum(margin, 0))
    moved = jax.random.randint(jax.random.fold_in(own, 4), (amount // 2,), 0, 1 << 20) % (margin + 1)
    lengths = lengths.at[donor].add(-moved).at[receiver].add(moved)
    items = jnp.searchsorted(jnp.cumsum(lengths), jnp.arange(rows * top), side="right").astype(jnp.int32)
    table = items.reshape(top, rows).T
    table = table[jax.random.permutation(jax.random.fold_in(own, 1), rows)]
    rotation = jax.random.randint(jax.random.fold_in(own, 2), (rows, 1), 0, top)
    return jnp.take_along_axis(table, (jnp.arange(top)[None, :] + rotation) % top, axis=1)


def portions_of(count, total, reach, lean, full):
    weights = [(1 << 20) // math.isqrt(standing ** lean) + 1 for standing in range(1, count + 1)]
    largest = reach if full else min(reach, max(-(-total // count), total * weights[0] // sum(weights)))
    least = 1 if total - largest >= count - 1 else 0
    holding, spare = [largest] + [least] * (count - 1), total - largest - least * (count - 1)
    while spare > 0:
        free = [i for i in range(1, count) if holding[i] < largest] or [i for i in range(1, count) if holding[i] < reach]
        whole, left = sum([weights[i] for i in free]), spare
        for i in free:
            more = min(reach - holding[i], max(1, left * weights[i] // whole), spare)
            holding[i] = holding[i] + more
            spare = spare - more
    return np.array(holding)


def bell_draw(rng, shape, width, bound, split=(), kind=jnp.bfloat16):
    array = width * jax.random.normal(rng, shape, jnp.float32)
    if split:
        array = array * level_of(rng, shape, split, -0.22, 0.18)
    return jnp.clip(array, -bound, bound).astype(kind)


def setup_inputs(seed: int = 0) -> dict:
    streams_of = jax.random.split(jax.random.key(seed), 14)
    residual_in = bell_draw(streams_of[0], (TOKENS, D), 1.0, 6.0, ((0, 32),))
    shortcut = bell_draw(streams_of[1], (TOKENS, D), 1.0, 6.0, ((0, 32),))
    attn_gain = jnp.clip(1.0 + 0.15 * jax.random.normal(streams_of[2], (D,), jnp.float32), 0.25, 1.75)
    moe_gain = jnp.clip(1.0 + 0.15 * jax.random.normal(streams_of[3], (D,), jnp.float32), 0.25, 1.75)
    query_weight = draw_query_weight(jax.random.fold_in(streams_of[13], 71), 0)
    key_value = draw_key_value(jax.random.fold_in(streams_of[13], 71), 0)
    output_weight = bell_draw(streams_of[6], (D, QH * HD), (QH * HD) ** -0.5, 0.09375, ((0, 32), (1, 8)))
    query_gain = draw_query_gain(jax.random.fold_in(streams_of[13], 71), 0)
    key_gain = draw_key_gain(jax.random.fold_in(streams_of[13], 71), 0)
    router_weight = bell_draw(streams_of[9], (EXPERTS, D), D ** -0.5, 0.125)
    expert_ids_keys = jax.random.split(jax.random.fold_in(streams_of[10], 1), TOKENS // ROWS)
    expert_ids_turns = jax.random.permutation(jax.random.fold_in(streams_of[10], 3), TOKENS // ROWS)
    expert_ids = jax.vmap(lambda own, number: routed_block(jax.random.fold_in(streams_of[10], 2), own, number, ROWS, EXPERTS, TOPK, CAP, 2))(expert_ids_keys, expert_ids_turns).reshape((TOKENS, TOPK))
    gate_up_weight = bell_draw(streams_of[11], (2 * EXPERTS, D, 2 * FF_DEV), D ** -0.5, 0.125, ((0, 256),))
    down_weight = bell_draw(streams_of[12], (2 * EXPERTS, FF_DEV, D), FF ** -0.5, 0.15625, ((0, 256),))
    return dict(residual_in=residual_in, shortcut=shortcut, attn_gain=attn_gain, moe_gain=moe_gain, query_weight=query_weight, key_value=key_value, output_weight=output_weight, query_gain=query_gain, key_gain=key_gain, router_weight=router_weight, expert_ids=expert_ids, gate_up_weight=gate_up_weight, down_weight=down_weight)


EPS = 1e-06
ROPE_BASE = 1000000.0

def norm_rows(values, gain):
    wide = values.astype(jnp.float32)
    return wide * lax.rsqrt(lax.optimization_barrier(jnp.mean(wide * wide, -1, keepdims=True)) + EPS) * gain.astype(jnp.float32)

def rotary(values):
    length = values.shape[0]
    half = values.shape[-1] // 2
    position = jnp.arange(length, dtype=jnp.float32)
    freq = ROPE_BASE ** (-jnp.arange(half, dtype=jnp.float32) * 2.0 / values.shape[-1])
    angle = position[:, None] * freq[None, :]
    cosine = jnp.cos(angle)[:, None, :]
    sine = jnp.sin(angle)[:, None, :]
    first = values[..., :half]
    second = values[..., half:]
    return jnp.concatenate([first * cosine - second * sine, second * cosine + first * sine], -1)

def reference(residual_in, shortcut, attn_gain, moe_gain, query_weight, key_value, output_weight, query_gain, key_gain, router_weight, expert_ids, gate_up_weight, down_weight):
    attn_rows = norm_rows(residual_in, attn_gain).astype(jnp.bfloat16)
    moe_rows = norm_rows(shortcut, moe_gain).astype(jnp.bfloat16)

    def one_sequence(rows):
        query = jnp.dot(rows, query_weight, preferred_element_type=jnp.float32).reshape(ROWS, QH, HD)
        query = rotary(norm_rows(query, query_gain)).astype(jnp.bfloat16).reshape(ROWS, KVH, GROUP, HD)
        keyval = jnp.dot(rows, key_value, preferred_element_type=jnp.float32).reshape(ROWS, 2, KVH, HD)
        keys = rotary(norm_rows(keyval[:, 0], key_gain)).astype(jnp.bfloat16)
        values = keyval[:, 1].astype(jnp.bfloat16)
        logits = jnp.einsum('sgjd,tgd->gjst', query.astype(jnp.float32), keys.astype(jnp.float32)) * HD ** (-0.5)
        causal = jnp.arange(ROWS)[:, None] >= jnp.arange(ROWS)[None, :]
        logits = jnp.where(causal, logits, -1e+30)
        peak = lax.optimization_barrier(jnp.max(logits, -1, keepdims=True))
        expo = jnp.exp(logits - peak)
        probs = (expo / lax.optimization_barrier(jnp.sum(expo, -1, keepdims=True))).astype(jnp.bfloat16)
        attended = jnp.einsum('gjst,tgd->sgjd', probs.astype(jnp.float32), values.astype(jnp.float32))
        attended = attended.astype(jnp.bfloat16).reshape(ROWS, N_TP, QH_DEV * HD)
        out_split = output_weight.reshape(D, N_TP, QH_DEV * HD)
        total = jnp.zeros((ROWS, D), jnp.float32)
        for index in range(N_TP):
            part = jnp.dot(attended[:, index], out_split[:, index].T, preferred_element_type=jnp.float32)
            total = total + lax.optimization_barrier(part.astype(jnp.bfloat16)).astype(jnp.float32)
        return total
    attention = lax.map(one_sequence, attn_rows.reshape(N_EP, ROWS, D)).reshape(TOKENS, D)
    logits_router = jnp.dot(moe_rows, router_weight.T, preferred_element_type=jnp.float32)
    chosen = jnp.take_along_axis(logits_router, expert_ids, axis=1)
    scores = jax.nn.sigmoid(chosen)
    gates = (scores / lax.optimization_barrier(jnp.sum(scores, 1, keepdims=True))).astype(jnp.bfloat16)
    hits = (expert_ids[:, :, None] == jnp.arange(EXPERTS, dtype=jnp.int32)[None, None, :]).astype(jnp.int32)
    per_row = lax.optimization_barrier(jnp.sum(hits, 1)).astype(jnp.int32).reshape(TOKENS // ROWS, ROWS, EXPERTS)
    earlier = (jnp.cumsum(per_row, 1).astype(jnp.int32) - per_row).reshape(TOKENS, EXPERTS)
    slot = jnp.take_along_axis(earlier, expert_ids, axis=1).astype(jnp.int32)
    device = (jnp.arange(TOKENS, dtype=jnp.int32) // ROWS)[:, None]
    place = (device * CAP + slot).astype(jnp.int32)
    buffer_rows = TOKENS // ROWS * CAP
    gate_up_split = gate_up_weight.reshape(EXPERTS, 2, D, 2 * FF_DEV)
    down_split = down_weight.reshape(EXPERTS, 2, FF_DEV, D)

    def one_expert(total, inputs):
        index, gate_up, down = inputs
        hit = expert_ids == index
        any_hit = jnp.any(hit, 1)
        summed_place = lax.optimization_barrier(jnp.sum(jnp.where(hit, place, 0), 1)).astype(jnp.int32)
        row_place = jnp.where(any_hit, summed_place, buffer_rows).astype(jnp.int32)
        buffer = jnp.zeros((buffer_rows, D), jnp.bfloat16).at[row_place].set(moe_rows, mode='drop')
        summed = jnp.zeros((buffer_rows, D), jnp.float32)
        for half in range(2):
            paired = jnp.dot(buffer, gate_up[half], preferred_element_type=jnp.float32)
            hidden = (jax.nn.silu(paired[:, :FF_DEV]) * paired[:, FF_DEV:]).astype(jnp.bfloat16)
            summed = summed + jnp.dot(hidden, down[half], preferred_element_type=jnp.float32)
        expert_out = summed.astype(jnp.bfloat16).astype(jnp.float32)
        weight = lax.optimization_barrier(jnp.sum(jnp.where(hit, gates.astype(jnp.float32), 0.0), 1))
        picked = expert_out[jnp.minimum(row_place, buffer_rows - 1)]
        return (total + weight[:, None] * picked, None)
    moe_out, _ = lax.scan(one_expert, jnp.zeros((TOKENS, D), jnp.float32), (jnp.arange(EXPERTS, dtype=jnp.int32), gate_up_split, down_split))
    return (residual_in.astype(jnp.float32) + attention + moe_out).astype(jnp.bfloat16)
```

```python
import functools

import jax
import jax.numpy as jnp
from jax import lax
from jax.experimental import pallas as pl
from jax.experimental.pallas import tpu as pltpu
from jax.sharding import PartitionSpec as P

HD = 128
QH = 32
KVH = 4
TOPK = 8
SLOTS = 16

EPS = 1e-06
ROPE_BASE = 1000000.0
F32 = jnp.float32
BF16 = jnp.bfloat16
NT = (((1,), (1,)), ((), ()))
VMEM_LIMIT = 48 * 1024 * 1024


def vmem():
    return pl.BlockSpec(memory_space=pltpu.VMEM)


def smem():
    return pl.BlockSpec(memory_space=pltpu.SMEM)


def call(body, out_shape, args, flops, extra_bytes=0, scratch=(), specs=None, out_specs=None):
    moved = sum(a.size * a.dtype.itemsize for a in args)
    moved += sum(o.size * o.dtype.itemsize for o in out_shape)
    return pl.pallas_call(
        body,
        out_shape=out_shape,
        in_specs=specs or [smem()] + [vmem()] * (len(args) - 1),
        out_specs=out_specs or [vmem()] * len(out_shape),
        scratch_shapes=list(scratch),
        compiler_params=pltpu.CompilerParams(vmem_limit_bytes=VMEM_LIMIT),
        cost_estimate=pl.CostEstimate(
            flops=flops, bytes_accessed=moved + extra_bytes, transcendentals=0
        ),
    )(*args)


def inverse_rms(wide):
    return lax.rsqrt(jnp.mean(wide * wide, -1, keepdims=True) + EPS)


def slots_of(ids_ref, experts):
    rows = ids_ref.shape[0]
    ids = ids_ref[...]
    lane = lax.broadcasted_iota(jnp.int32, (rows, experts), 1)
    hit = ids[:, 0:1] == lane
    for k in range(1, TOPK):
        hit = hit | (ids[:, k : k + 1] == lane)
    below = lax.broadcasted_iota(jnp.int32, (rows, rows), 0)
    above = lax.broadcasted_iota(jnp.int32, (rows, rows), 1)
    lower = jnp.where(below > above, 1.0, 0.0).astype(BF16)
    earlier = jnp.dot(lower, jnp.where(hit, 1.0, 0.0).astype(BF16), preferred_element_type=F32)
    return hit, jnp.where(hit, earlier, -1.0).astype(BF16)


def dispatch_body(rank_ref, rows_ref, gain_ref, ids_ref, out_ref):
    rank = rank_ref[0]
    group, side = rank // 2, rank % 2
    width = out_ref.shape[1]
    places = out_ref.shape[0]
    experts = places // SLOTS * 4
    _, slot = slots_of(ids_ref, experts)
    place = lax.broadcasted_iota(jnp.int32, (places, experts), 0)
    expert = lax.broadcasted_iota(jnp.int32, (places, experts), 1)
    pick = jnp.where(expert == place // SLOTS * 4 + group, 1.0, 0.0).astype(BF16)
    spread = lax.dot_general(pick, slot, NT, preferred_element_type=F32)
    wanted = lax.broadcasted_iota(jnp.int32, spread.shape, 0) % SLOTS
    chosen = jnp.where(spread == wanted.astype(F32), 1.0, 0.0).astype(BF16)
    scale = inverse_rms(rows_ref[...].astype(F32))
    start = pl.multiple_of(side * width, width)
    half = rows_ref[:, pl.ds(start, width)].astype(F32)
    normed = (half * scale * gain_ref[:, pl.ds(start, width)]).astype(BF16)
    out_ref[...] = jnp.dot(chosen, normed, preferred_element_type=F32).astype(BF16)


def combine_map_body(rank_ref, rows_ref, gain_ref, router_ref, ids_ref, out_ref):
    group = rank_ref[0] // 2
    places = out_ref.shape[1]
    experts = router_ref.shape[0]
    hit, slot = slots_of(ids_ref, experts)
    wide = rows_ref[...].astype(F32)
    normed = (wide * inverse_rms(wide) * gain_ref[...]).astype(BF16)
    logits = lax.dot_general(normed, router_ref[...], NT, preferred_element_type=F32)
    scores = jnp.where(hit, jax.nn.sigmoid(logits), 0.0)
    gates = (scores / jnp.sum(scores, -1, keepdims=True)).astype(BF16)
    expert = lax.broadcasted_iota(jnp.int32, (experts, places), 0)
    place = lax.broadcasted_iota(jnp.int32, (experts, places), 1)
    pick = jnp.where(expert == place // SLOTS * 4 + group, 1.0, 0.0).astype(BF16)
    spread = jnp.dot(slot, pick, preferred_element_type=F32)
    gate = jnp.dot(gates, pick, preferred_element_type=F32)
    wanted = lax.broadcasted_iota(jnp.int32, spread.shape, 1) % SLOTS
    out_ref[...] = jnp.where(spread == wanted.astype(F32), gate, 0.0).astype(BF16)


def first_half_body(rank_ref, x_ref, w_ref, out_ref):
    out_ref[...] = jnp.dot(x_ref[...], w_ref[0], preferred_element_type=F32)


def expert_body(rank_ref, acc_ref, x_ref, w_ref, down_ref, kept_ref, handed_ref):
    side = rank_ref[0] % 2
    paired = acc_ref[...] + jnp.dot(x_ref[...], w_ref[0], preferred_element_type=F32)
    ff = paired.shape[1] // 2
    hidden = (jax.nn.silu(paired[:, :ff]) * paired[:, ff:]).astype(BF16)
    width = kept_ref.shape[1]
    mine = pl.multiple_of(side * width, width)
    other = pl.multiple_of((1 - side) * width, width)
    handed_ref[...] = jnp.dot(
        hidden, down_ref[0, :, pl.ds(other, width)], preferred_element_type=F32
    ).astype(BF16)
    kept_ref[...] = jnp.dot(
        hidden, down_ref[0, :, pl.ds(mine, width)], preferred_element_type=F32
    )


def attention_body(
    rank_ref, rows_ref, gain_ref, w_ref, qg_ref, kg_ref, cos_ref, sin_ref, kept_ref, handed_ref
):
    side = rank_ref[0] % 2
    seq = rows_ref.shape[0]
    heads = (w_ref.shape[1] // HD - 2) // 2
    wide = rows_ref[...].astype(F32)
    normed = (wide * inverse_rms(wide) * gain_ref[...]).astype(BF16)
    columns = (heads + 2) * HD
    qkv = jnp.dot(normed, w_ref[:, :columns], preferred_element_type=F32)
    cosine, sine = cos_ref[...], sin_ref[...]

    def turned(values, gain):
        values = values * inverse_rms(values) * gain
        return (values * cosine + pltpu.roll(values, HD // 2, 1) * sine).astype(BF16)

    keys = turned(qkv[:, heads * HD : (heads + 1) * HD], kg_ref[...])
    values = qkv[:, (heads + 1) * HD :].astype(BF16)
    below = lax.broadcasted_iota(jnp.int32, (seq, seq), 0)
    above = lax.broadcasted_iota(jnp.int32, (seq, seq), 1)
    causal = below >= above
    parts = []
    for head in range(heads):
        query = turned(qkv[:, head * HD : (head + 1) * HD], qg_ref[...])
        logits = lax.dot_general(query, keys, NT, preferred_element_type=F32) * HD**-0.5
        logits = jnp.where(causal, logits, -1e30)
        expo = jnp.exp(logits - jnp.max(logits, -1, keepdims=True))
        probs = (expo / jnp.sum(expo, -1, keepdims=True)).astype(BF16)
        parts.append(jnp.dot(probs, values, preferred_element_type=F32).astype(BF16))
    attended = jnp.concatenate(parts, 1)
    width = kept_ref.shape[1]
    mine = pl.multiple_of(side * width, width)
    other = pl.multiple_of((1 - side) * width, width)
    handed_ref[...] = lax.dot_general(
        attended, w_ref[pl.ds(other, width), columns:], NT, preferred_element_type=F32
    ).astype(BF16)
    kept_ref[...] = lax.dot_general(
        attended, w_ref[pl.ds(mine, width), columns:], NT, preferred_element_type=F32
    )


def combine_body(map_ref, back_ref, kept_ref, got_ref, out_ref):
    total = jnp.dot(map_ref[...], back_ref[...], preferred_element_type=F32)
    out_ref[...] = (total + kept_ref[...] + got_ref[...].astype(F32)).astype(BF16)


def local(
    residual_in,
    shortcut,
    attn_gain,
    moe_gain,
    query_weight,
    key_value,
    output_weight,
    query_gain,
    key_gain,
    router_weight,
    expert_ids,
    gate_up_weight,
    down_weight,
):
    n_ep = lax.axis_size("ep")
    n_tp = lax.axis_size("tp")
    rank = lax.axis_index("tp")
    ranks = rank.astype(jnp.int32)[None]
    side = rank % 2
    group_id = rank // 2
    pairs = n_tp // 2
    rows, d_model = residual_in.shape
    half = d_model // 2
    places = n_ep * SLOTS
    ff2 = gate_up_weight.shape[2]
    ff = ff2 // 2
    qh_dev = query_weight.shape[1] // HD
    kv_head = rank * qh_dev // (QH // KVH)
    partner = [(i, i ^ 1) for i in range(n_tp)]
    sides = [[2 * i + h for i in range(pairs)] for h in range(2)]

    own_key = lax.dynamic_slice_in_dim(key_value, kv_head * HD, HD, 1)
    own_value = lax.dynamic_slice_in_dim(key_value, (KVH + kv_head) * HD, HD, 1)
    packed = jnp.concatenate([query_weight, own_key, own_value, output_weight], 1)
    weights = lax.all_gather(packed, "ep", axis=0, tiled=True)

    moe_gain = moe_gain[None, :]
    (outgoing,) = call(
        dispatch_body,
        [jax.ShapeDtypeStruct((places, half), BF16)],
        (ranks, shortcut, moe_gain, expert_ids),
        2 * places * rows * half,
    )
    arrived = lax.all_to_all(outgoing, "ep", split_axis=0, concat_axis=0, tiled=True)
    (combine,) = call(
        combine_map_body,
        [jax.ShapeDtypeStruct((rows, places), BF16)],
        (ranks, shortcut, moe_gain, router_weight, expert_ids),
        2 * rows * 128 * d_model,
    )
    received = lax.ppermute(arrived, "tp", partner)

    def chosen_half(which):
        return pl.BlockSpec((1, half, ff2), lambda i, rank_ref: (0, which(rank_ref[0] % 2), 0))

    def whole(shape):
        return pl.BlockSpec(shape, lambda i, rank_ref: (0,) * len(shape))

    (acc,) = pl.pallas_call(
        first_half_body,
        out_shape=[jax.ShapeDtypeStruct((places, ff2), F32)],
        grid_spec=pltpu.PrefetchScalarGridSpec(
            num_scalar_prefetch=1,
            grid=(1,),
            in_specs=[whole((places, half)), chosen_half(lambda s: s)],
            out_specs=[whole((places, ff2))],
        ),
        compiler_params=pltpu.CompilerParams(vmem_limit_bytes=VMEM_LIMIT),
        cost_estimate=pl.CostEstimate(
            flops=2 * places * half * ff2, bytes_accessed=half * ff2 * 2 + places * ff2 * 4, transcendentals=0
        ),
    )(ranks, arrived, gate_up_weight)
    kept, handed = pl.pallas_call(
        expert_body,
        out_shape=[
            jax.ShapeDtypeStruct((places, half), F32),
            jax.ShapeDtypeStruct((places, half), BF16),
        ],
        grid_spec=pltpu.PrefetchScalarGridSpec(
            num_scalar_prefetch=1,
            grid=(1,),
            in_specs=[
                whole((places, ff2)),
                whole((places, half)),
                chosen_half(lambda s: 1 - s),
                whole((1, ff, d_model)),
            ],
            out_specs=[whole((places, half)), whole((places, half))],
        ),
        compiler_params=pltpu.CompilerParams(vmem_limit_bytes=VMEM_LIMIT),
        cost_estimate=pl.CostEstimate(
            flops=2 * places * half * ff2 + 2 * places * ff * d_model,
            bytes_accessed=half * ff2 * 2 + places * ff2 * 4 + ff * d_model * 2,
            transcendentals=0,
        ),
    )(ranks, acc, received, gate_up_weight, down_weight)
    got = lax.ppermute(handed, "tp", partner)
    expert_out = (kept + got.astype(F32)).astype(BF16)
    returned = lax.all_to_all(expert_out, "ep", split_axis=0, concat_axis=0, tiled=True)

    position = jnp.arange(rows, dtype=F32)
    freq = ROPE_BASE ** (-jnp.arange(HD // 2, dtype=F32) * 2.0 / HD)
    angle = position[:, None] * freq[None, :]
    cosine, sine = jnp.cos(angle), jnp.sin(angle)
    cosine = jnp.concatenate([cosine, cosine], 1)
    sine = jnp.concatenate([-sine, sine], 1)
    att_kept, att_handed = call(
        attention_body,
        [jax.ShapeDtypeStruct((rows, half), F32), jax.ShapeDtypeStruct((rows, half), BF16)],
        (
            ranks,
            residual_in,
            attn_gain[None, :],
            weights,
            query_gain[None, :],
            key_gain[None, :],
            cosine,
            sine,
        ),
        2 * rows * d_model * weights.shape[1],
    )
    att_got = lax.ppermute(att_handed, "tp", partner)
    (total,) = call(
        combine_body,
        [jax.ShapeDtypeStruct((rows, half), BF16)],
        (combine, returned, att_kept, att_got),
        2 * rows * places * half,
        specs=[vmem()] * 4,
    )
    terms = lax.all_to_all(
        total.reshape(pairs, rows // pairs, half),
        "tp",
        split_axis=0,
        concat_axis=0,
        tiled=True,
        axis_index_groups=sides,
    )
    share = rows // pairs
    own = lax.dynamic_slice(residual_in, (group_id * share, side * half), (share, half))
    mine = (own.astype(F32) + jnp.sum(terms.astype(F32), 0)).astype(BF16)
    everyone = lax.all_to_all(
        jnp.broadcast_to(mine[None], (n_tp, share, half)), "tp", split_axis=0, concat_axis=0, tiled=True
    )
    return everyone.reshape(pairs, 2, share, half).transpose(0, 2, 1, 3).reshape(rows, d_model)


def solution(mesh):
    return jax.shard_map(
        local,
        mesh=mesh,
        in_specs=(
            P("ep", None),
            P("ep", None),
            P(),
            P(),
            P("ep", "tp"),
            P("ep", None),
            P("ep", "tp"),
            P(),
            P(),
            P(),
            P("ep", None),
            P(("ep", "tp"), None, None),
            P(("ep", "tp"), None, None),
        ),
        out_specs=P("ep", None),
        check_vma=False,
    )
```

```python
import functools

import jax
import jax.numpy as jnp
from jax import lax
from jax.experimental import pallas as pl
from jax.experimental.pallas import tpu as pltpu
from jax.sharding import PartitionSpec as P

HD = 128
QH = 32
KVH = 4
TOPK = 8
SLOTS = 16

EPS = 1e-06
ROPE_BASE = 1000000.0
F32 = jnp.float32
BF16 = jnp.bfloat16
NT = (((1,), (1,)), ((), ()))
VMEM_LIMIT = 56 * 1024 * 1024


def vmem():
    return pl.BlockSpec(memory_space=pltpu.VMEM)


def anywhere():
    return pl.BlockSpec(memory_space=pl.ANY)


def call(body, out_shape, args, flops, extra_bytes=0, scratch=(), specs=None, out_specs=None, aliases=None, cost=None):
    moved = extra_bytes + sum(a.size * a.dtype.itemsize for a in args)
    moved += sum(o.size * o.dtype.itemsize for o in out_shape)
    return pl.pallas_call(
        body,
        out_shape=out_shape,
        in_specs=specs or [vmem()] * len(args),
        out_specs=out_specs or [vmem()] * len(out_shape),
        scratch_shapes=list(scratch),
        input_output_aliases=aliases or {},
        compiler_params=pltpu.CompilerParams(vmem_limit_bytes=VMEM_LIMIT),
        cost_estimate=pl.CostEstimate(
            flops=flops if cost is None else cost,
            bytes_accessed=moved if cost is None else cost,
            transcendentals=0,
        ),
    )(*args)


def inverse_rms(wide):
    return lax.rsqrt(jnp.mean(wide * wide, -1, keepdims=True) + EPS)


def slots_of(ids_ref, experts):
    rows = ids_ref.shape[1]
    expert = lax.broadcasted_iota(jnp.int32, (experts, rows), 0)
    hit = ids_ref[0:1, :] == expert
    for k in range(1, TOPK):
        hit = hit | (ids_ref[k : k + 1, :] == expert)
    before = lax.broadcasted_iota(jnp.int32, (rows, rows), 0)
    after = lax.broadcasted_iota(jnp.int32, (rows, rows), 1)
    upper = jnp.where(before < after, 1.0, 0.0).astype(BF16)
    earlier = jnp.dot(jnp.where(hit, 1.0, 0.0).astype(BF16), upper, preferred_element_type=F32)
    slot = jnp.where(hit, earlier, -1.0).astype(BF16)
    places = experts // 4 * SLOTS
    place = lax.broadcasted_iota(jnp.int32, (places, experts), 0)
    column = lax.broadcasted_iota(jnp.int32, (places, experts), 1)
    group = lax.axis_index("tp") // 2
    pick = jnp.where(column == place // SLOTS * 4 + group, 1.0, 0.0).astype(BF16)
    spread = jnp.dot(pick, slot, preferred_element_type=F32)
    wanted = lax.broadcasted_iota(jnp.int32, spread.shape, 0) % SLOTS
    return hit, pick, spread == wanted.astype(F32)


def dispatch_body(rows_ref, gain_ref, ids_ref, shared_ref, direct_ref):
    side = lax.axis_index("tp") % 2
    places, width = shared_ref.shape
    _, _, filled = slots_of(ids_ref, places // SLOTS * 4)
    chosen = jnp.where(filled, 1.0, 0.0).astype(BF16)
    scale = inverse_rms(rows_ref[...].astype(F32))

    def place_columns(columns, out_ref):
        part = rows_ref[:, columns].astype(F32)
        normed = (part * scale * gain_ref[:, columns]).astype(BF16)
        out_ref[...] = jnp.dot(chosen, normed, preferred_element_type=F32).astype(BF16)

    place_columns(pl.ds(pl.multiple_of(side * width, width), width), shared_ref)
    place_columns(pl.ds(2 * width, direct_ref.shape[1]), direct_ref)


def combine_map_body(rows_ref, gain_ref, router_ref, ids_ref, out_ref):
    hit, pick, filled = slots_of(ids_ref, router_ref.shape[0])
    wide = rows_ref[...].astype(F32)
    normed = (wide * inverse_rms(wide) * gain_ref[...]).astype(BF16)
    logits = lax.dot_general(router_ref[...], normed, NT, preferred_element_type=F32)
    scores = jnp.where(hit, jax.nn.sigmoid(logits), 0.0)
    gates = (scores / jnp.sum(scores, 0, keepdims=True)).astype(BF16)
    gate = jnp.dot(pick, gates, preferred_element_type=F32)
    out_ref[...] = jnp.where(filled, gate, 0.0).T.astype(BF16)


def relay_body(value_ref, after_ref, out_ref):
    pass


def first_part_body(own_ref, w_ref, out_ref, w_buf, sem):
    width = own_ref.shape[1]
    mine = pl.multiple_of(lax.axis_index("tp") % 2 * width, width)
    copy = pltpu.make_async_copy(w_ref.at[0, pl.ds(mine, width)], w_buf, sem)
    copy.start()
    copy.wait()
    out_ref[...] = jnp.dot(own_ref[...], w_buf[...], preferred_element_type=F32)


def expert_body(
    acc_ref,
    got_ref,
    both_ref,
    w_ref,
    down_ref,
    near_ref,
    direct_ref,
    handed_ref,
    kept_ref,
    acc,
    x_buf,
    w_buf,
    w_down,
    hidden,
    out_direct,
    out_handed,
    out_kept,
    sems,
):
    side = lax.axis_index("tp") % 2
    width = out_kept.shape[1]
    mine = pl.multiple_of(side * width, width)
    other = pl.multiple_of((1 - side) * width, width)
    ff = hidden.shape[1]
    tile = 256
    moves = [
        (got_ref, x_buf.at[:, :width]),
        (both_ref, x_buf.at[:, width:]),
    ]
    for start in (0, ff):
        columns = pl.ds(start, ff)
        moves.append((w_ref.at[0, pl.ds(other, width), columns], w_buf.at[:width, columns]))
        moves.append((w_ref.at[0, 2 * width :, columns], w_buf.at[width:, columns]))
    moves.append((acc_ref, acc))
    moves.append((down_ref.at[0], w_down))
    copies = [pltpu.make_async_copy(a, b, sems.at[i]) for i, (a, b) in enumerate(moves)]
    for copy in copies:
        copy.start()
    for copy in copies[:-1]:
        copy.wait()
    x = x_buf[...]
    for at in range(0, ff, tile):
        gate = acc[:, at : at + tile] + jnp.dot(
            x, w_buf[:, at : at + tile], preferred_element_type=F32
        )
        up = acc[:, ff + at : ff + at + tile] + jnp.dot(
            x, w_buf[:, ff + at : ff + at + tile], preferred_element_type=F32
        )
        hidden[:, at : at + tile] = (jax.nn.silu(gate) * up).astype(BF16)
    copies[-1].wait()

    def projected(columns):
        return jnp.dot(hidden[...], w_down[:, columns], preferred_element_type=F32).astype(BF16)

    out_handed[...] = projected(pl.ds(other, width))
    back = [pltpu.make_async_copy(out_handed, handed_ref, sems.at[8])]
    back[0].start()
    out_direct[...] = projected(pl.ds(2 * width, out_direct.shape[1]))
    back.append(pltpu.make_async_copy(out_direct, direct_ref, sems.at[9]))
    back[1].start()
    out_kept[...] = projected(pl.ds(mine, width))
    back.append(pltpu.make_async_copy(out_kept, kept_ref, sems.at[10]))
    back[2].start()
    for copy in back:
        copy.wait()


def attention_body(
    rows_ref,
    gain_ref,
    near_ref,
    across_ref,
    other_near_ref,
    other_across_ref,
    qg_ref,
    kg_ref,
    cos_ref,
    sin_ref,
    handed_ref,
    kept_ref,
    direct_ref,
    w_ref,
):
    side = lax.axis_index("tp") % 2
    place = lax.axis_index("ep")
    along, core = place // 16, place % 2
    sources = (
        (near_ref, along, core),
        (across_ref, 1 - along, core),
        (other_near_ref, along, 1 - core),
        (other_across_ref, 1 - along, 1 - core),
    )
    block = w_ref.shape[0] // 32
    for ref, x_at, core_at in sources:
        for z in range(8):
            start = pl.multiple_of(((x_at * 8 + z) * 2 + core_at) * block, block)
            w_ref[pl.ds(start, block), :] = ref[z * block : (z + 1) * block, :]
    seq = rows_ref.shape[0]
    heads = (w_ref.shape[1] // HD - 2) // 2
    wide = rows_ref[...].astype(F32)
    normed = (wide * inverse_rms(wide) * gain_ref[...]).astype(BF16)
    columns = (heads + 2) * HD
    qkv = jnp.dot(normed, w_ref[:, :columns], preferred_element_type=F32)
    cosine, sine = cos_ref[...], sin_ref[...]

    def turned(values, gain):
        values = values * inverse_rms(values) * gain
        return (values * cosine + pltpu.roll(values, HD // 2, 1) * sine).astype(BF16)

    keys = turned(qkv[:, heads * HD : (heads + 1) * HD], kg_ref[...])
    values = qkv[:, (heads + 1) * HD :].astype(BF16)
    below = lax.broadcasted_iota(jnp.int32, (seq, seq), 0)
    above = lax.broadcasted_iota(jnp.int32, (seq, seq), 1)
    causal = below >= above
    parts = []
    for head in range(heads):
        query = turned(qkv[:, head * HD : (head + 1) * HD], qg_ref[...])
        logits = lax.dot_general(query, keys, NT, preferred_element_type=F32) * HD**-0.5
        logits = jnp.where(causal, logits, -1e30)
        expo = jnp.exp(logits - jnp.max(logits, -1, keepdims=True))
        probs = (expo / jnp.sum(expo, -1, keepdims=True)).astype(BF16)
        parts.append(jnp.dot(probs, values, preferred_element_type=F32).astype(BF16))
    attended = jnp.concatenate(parts, 1)
    width = kept_ref.shape[1]
    mine = pl.multiple_of(side * width, width)
    other = pl.multiple_of((1 - side) * width, width)
    handed_ref[...] = lax.dot_general(
        attended, w_ref[pl.ds(other, width), columns:], NT, preferred_element_type=F32
    ).astype(BF16)
    kept_ref[...] = lax.dot_general(
        attended, w_ref[pl.ds(mine, width), columns:], NT, preferred_element_type=F32
    )
    direct_ref[...] = lax.dot_general(
        attended, w_ref[2 * width :, columns:], NT, preferred_element_type=F32
    )


def combine_body(map_ref, shared_ref, both_ref, kept_ref, got_ref, direct_ref, out_ref):
    width = kept_ref.shape[1]
    shared = jnp.dot(map_ref[...], shared_ref[...], preferred_element_type=F32)
    out_ref[:, :width] = (shared + kept_ref[...] + got_ref[...].astype(F32)).astype(BF16)
    both = jnp.dot(map_ref[...], both_ref[...], preferred_element_type=F32)
    out_ref[:, width:] = (both + direct_ref[...]).astype(BF16)


def local(
    residual_in,
    shortcut,
    attn_gain,
    moe_gain,
    query_weight,
    key_value,
    output_weight,
    query_gain,
    key_gain,
    router_weight,
    expert_ids,
    gate_up_weight,
    down_weight,
):
    n_ep = lax.axis_size("ep")
    n_tp = lax.axis_size("tp")
    rank = lax.axis_index("tp")
    rows, d_model = residual_in.shape
    direct = d_model // 4
    shared = (d_model - direct) // 2
    places = n_ep * SLOTS
    ff2 = gate_up_weight.shape[2]
    ff = ff2 // 2
    qh_dev = query_weight.shape[1] // HD
    kv_head = rank * qh_dev // (QH // KVH)
    along_z = [[x * 16 + z * 2 + c for z in range(8)] for x in range(2) for c in range(2)]
    partner = [(i, i ^ 1) for i in range(n_tp)]

    own_key = lax.dynamic_slice_in_dim(key_value, kv_head * HD, HD, 1)
    own_value = lax.dynamic_slice_in_dim(key_value, (KVH + kv_head) * HD, HD, 1)
    packed = jnp.concatenate([query_weight, own_key, own_value, output_weight], 1)
    near = lax.all_gather(packed, "ep", axis=0, tiled=True, axis_index_groups=along_z)

    def to_owners(value):
        return lax.all_to_all(value, "ep", split_axis=0, concat_axis=0, tiled=True)

    def swapped(value):
        return lax.ppermute(value, "tp", partner)

    moe_gain = moe_gain[None, :]
    ids = expert_ids.T
    outgoing, outgoing_both = call(
        dispatch_body,
        [
            jax.ShapeDtypeStruct((places, shared), BF16),
            jax.ShapeDtypeStruct((places, direct), BF16),
        ],
        (shortcut, moe_gain, ids),
        2 * places * rows * (shared + direct),
    )
    arrived = to_owners(outgoing)
    received = swapped(arrived)
    arrived_both = to_owners(outgoing_both)
    (combine,) = call(
        combine_map_body,
        [jax.ShapeDtypeStruct((rows, places), BF16)],
        (shortcut, moe_gain, router_weight, ids),
        2 * rows * 128 * d_model,
        cost=0,
    )
    (acc,) = call(
        first_part_body,
        [jax.ShapeDtypeStruct((places, ff2), F32)],
        (arrived, gate_up_weight),
        2 * places * shared * ff2,
        specs=[vmem(), anywhere()],
        scratch=[pltpu.VMEM((shared, ff2), BF16), pltpu.SemaphoreType.DMA],
    )
    out_both, handed, kept = call(
        expert_body,
        [
            jax.ShapeDtypeStruct((places, direct), BF16),
            jax.ShapeDtypeStruct((places, shared), BF16),
            jax.ShapeDtypeStruct((places, shared), BF16),
        ],
        (acc, received, arrived_both, gate_up_weight, down_weight, near),
        2 * places * (shared + direct) * ff2 + 2 * places * ff * d_model,
        specs=[anywhere()] * 6,
        out_specs=[anywhere()] * 3,
        scratch=[
            pltpu.VMEM((places, ff2), F32),
            pltpu.VMEM((places, shared + direct), BF16),
            pltpu.VMEM((shared + direct, ff2), BF16),
            pltpu.VMEM((ff, d_model), BF16),
            pltpu.VMEM((places, ff), BF16),
            pltpu.VMEM((places, direct), BF16),
            pltpu.VMEM((places, shared), BF16),
            pltpu.VMEM((places, shared), BF16),
            pltpu.SemaphoreType.DMA((11,)),
        ],
    )
    across = lax.ppermute(near, "ep", [(i, i ^ 16) for i in range(n_ep)])
    cores = [(i, i ^ 1) for i in range(n_ep)]
    other_near = lax.ppermute(near, "ep", cores)
    got = swapped(handed)
    returned_both = to_owners(out_both)
    expert_out = (kept.astype(F32) + got.astype(F32)).astype(BF16)
    returned = to_owners(expert_out)
    (across,) = call(
        relay_body,
        [jax.ShapeDtypeStruct(across.shape, BF16)],
        (across, expert_out),
        0,
        cost=0,
        specs=[anywhere()] * 2,
        out_specs=[anywhere()],
        aliases={0: 0},
    )
    other_across = lax.ppermute(across, "ep", cores)

    position = jnp.arange(rows, dtype=F32)
    freq = ROPE_BASE ** (-jnp.arange(HD // 2, dtype=F32) * 2.0 / HD)
    angle = position[:, None] * freq[None, :]
    cosine, sine = jnp.cos(angle), jnp.sin(angle)
    cosine = jnp.concatenate([cosine, cosine], 1)
    sine = jnp.concatenate([-sine, sine], 1)
    att_handed, att_kept, att_both = call(
        attention_body,
        [
            jax.ShapeDtypeStruct((rows, shared), BF16),
            jax.ShapeDtypeStruct((rows, shared), F32),
            jax.ShapeDtypeStruct((rows, direct), F32),
        ],
        (
            residual_in,
            attn_gain[None, :],
            near,
            across,
            other_near,
            other_across,
            query_gain[None, :],
            key_gain[None, :],
            cosine,
            sine,
        ),
        2 * rows * d_model * packed.shape[1],
        cost=0,
        scratch=[pltpu.VMEM((d_model, packed.shape[1]), BF16)],
    )
    att_got = swapped(att_handed)
    (total,) = call(
        combine_body,
        [jax.ShapeDtypeStruct((rows, shared + direct), BF16)],
        (combine, returned, returned_both, att_kept, att_got, att_both),
        2 * rows * places * (shared + direct),
        specs=[vmem()] * 6,
    )
    share = rows // n_tp
    terms = lax.all_to_all(
        total.reshape(n_tp, share, shared + direct),
        "tp",
        split_axis=0,
        concat_axis=0,
        tiled=True,
    )
    terms = terms.astype(F32)
    sums = [jnp.sum(terms[h::2, :, :shared], 0) for h in range(2)]
    sums = jnp.concatenate(sums + [jnp.sum(terms[:, :, shared:], 0)], 1)
    own = lax.dynamic_slice_in_dim(residual_in, rank * share, share, 0)
    mine = (own.astype(F32) + sums).astype(BF16)
    everyone = lax.all_to_all(
        jnp.broadcast_to(mine[None], (n_tp, share, d_model)),
        "tp",
        split_axis=0,
        concat_axis=0,
        tiled=True,
    )
    return everyone.reshape(rows, d_model)


def solution(mesh):
    return jax.shard_map(
        local,
        mesh=mesh,
        in_specs=(
            P("ep", None),
            P("ep", None),
            P(),
            P(),
            P("ep", "tp"),
            P("ep", None),
            P("ep", "tp"),
            P(),
            P(),
            P(),
            P("ep", None),
            P(("ep", "tp"), None, None),
            P(("ep", "tp"), None, None),
        ),
        out_specs=P("ep", None),
        check_vma=False,
    )
```

```python
import functools

import jax
import jax.numpy as jnp
from jax import lax
from jax.experimental import pallas as pl
from jax.experimental.pallas import tpu as pltpu
from jax.sharding import PartitionSpec as P

HD = 128
QH = 32
KVH = 4
TOPK = 8
SLOTS = 16

EPS = 1e-06
ROPE_BASE = 1000000.0
F32 = jnp.float32
BF16 = jnp.bfloat16
NT = (((1,), (1,)), ((), ()))


def vmem():
    return pl.BlockSpec(memory_space=pltpu.VMEM)


def anywhere():
    return pl.BlockSpec(memory_space=pl.ANY)


def call(body, out_shape, args, flops, extra_bytes=0, scratch=(), specs=None, out_specs=None, aliases=None, cost=None, limit=56):
    moved = extra_bytes + sum(a.size * a.dtype.itemsize for a in args)
    moved += sum(o.size * o.dtype.itemsize for o in out_shape)
    return pl.pallas_call(
        body,
        out_shape=out_shape,
        in_specs=specs or [vmem()] * len(args),
        out_specs=out_specs or [vmem()] * len(out_shape),
        scratch_shapes=list(scratch),
        input_output_aliases=aliases or {},
        compiler_params=pltpu.CompilerParams(vmem_limit_bytes=limit * 1024 * 1024),
        cost_estimate=pl.CostEstimate(
            flops=flops if cost is None else cost,
            bytes_accessed=moved if cost is None else cost,
            transcendentals=0,
        ),
    )(*args)


def inverse_rms(wide):
    return lax.rsqrt(jnp.mean(wide * wide, -1, keepdims=True) + EPS)


def slots_of(ids_ref, experts):
    rows = ids_ref.shape[1]
    expert = lax.broadcasted_iota(jnp.int32, (experts, rows), 0)
    hit = ids_ref[0:1, :] == expert
    for k in range(1, TOPK):
        hit = hit | (ids_ref[k : k + 1, :] == expert)
    before = lax.broadcasted_iota(jnp.int32, (rows, rows), 0)
    after = lax.broadcasted_iota(jnp.int32, (rows, rows), 1)
    upper = jnp.where(before < after, 1.0, 0.0).astype(BF16)
    earlier = jnp.dot(jnp.where(hit, 1.0, 0.0).astype(BF16), upper, preferred_element_type=F32)
    slot = jnp.where(hit, earlier, -1.0).astype(BF16)
    places = experts // 4 * SLOTS
    place = lax.broadcasted_iota(jnp.int32, (places, experts), 0)
    column = lax.broadcasted_iota(jnp.int32, (places, experts), 1)
    group = lax.axis_index("tp") // 2
    pick = jnp.where(column == place // SLOTS * 4 + group, 1.0, 0.0).astype(BF16)
    spread = jnp.dot(pick, slot, preferred_element_type=F32)
    wanted = lax.broadcasted_iota(jnp.int32, spread.shape, 0) % SLOTS
    return hit, pick, spread == wanted.astype(F32)


def dispatch_body(rows_ref, gain_ref, ids_ref, shared_ref, direct_ref):
    side = lax.axis_index("tp") % 2
    places, width = shared_ref.shape
    _, _, filled = slots_of(ids_ref, places // SLOTS * 4)
    chosen = jnp.where(filled, 1.0, 0.0).astype(BF16)
    scale = inverse_rms(rows_ref[...].astype(F32))

    def place_columns(columns, out_ref):
        part = rows_ref[:, columns].astype(F32)
        normed = (part * scale * gain_ref[:, columns]).astype(BF16)
        out_ref[...] = jnp.dot(chosen, normed, preferred_element_type=F32).astype(BF16)

    place_columns(pl.ds(pl.multiple_of(side * width, width), width), shared_ref)
    place_columns(pl.ds(2 * width, direct_ref.shape[1]), direct_ref)


def combine_map_body(rows_ref, gain_ref, router_ref, ids_ref, out_ref):
    hit, pick, filled = slots_of(ids_ref, router_ref.shape[0])
    wide = rows_ref[...].astype(F32)
    normed = (wide * inverse_rms(wide) * gain_ref[...]).astype(BF16)
    logits = lax.dot_general(router_ref[...], normed, NT, preferred_element_type=F32)
    scores = jnp.where(hit, jax.nn.sigmoid(logits), 0.0)
    gates = (scores / jnp.sum(scores, 0, keepdims=True)).astype(BF16)
    gate = jnp.dot(pick, gates, preferred_element_type=F32)
    out_ref[...] = jnp.where(filled, gate, 0.0).T.astype(BF16)


def relay_body(value_ref, after_ref, out_ref):
    pass


def first_part_body(own_ref, w_ref, out_ref, w_buf, sem):
    width = own_ref.shape[1]
    mine = pl.multiple_of(lax.axis_index("tp") % 2 * width, width)
    copy = pltpu.make_async_copy(w_ref.at[0, pl.ds(mine, width)], w_buf, sem)
    copy.start()
    copy.wait()
    out_ref[...] = jnp.dot(own_ref[...], w_buf[...], preferred_element_type=F32)


def expert_body(
    acc_ref,
    got_ref,
    both_ref,
    w_ref,
    down_ref,
    near_ref,
    direct_ref,
    handed_ref,
    kept_ref,
    acc,
    x_buf,
    w_buf,
    w_down,
    hidden,
    out_direct,
    out_handed,
    out_kept,
    sems,
):
    side = lax.axis_index("tp") % 2
    used = iter(range(32))

    def started(source, target):
        copy = pltpu.make_async_copy(source, target, sems.at[next(used)])
        copy.start()
        return copy

    width = got_ref.shape[1]
    other = pl.multiple_of((1 - side) * width, width)
    ff = hidden.shape[1]
    tile = 256
    inputs = [started(got_ref, x_buf.at[:, :width]), started(both_ref, x_buf.at[:, width:])]
    strips = []
    for at in range(0, ff, tile):
        strip = []
        for start in (at, ff + at):
            columns = pl.ds(start, tile)
            strip += [
                started(w_ref.at[0, pl.ds(other, width), columns], w_buf.at[:width, columns]),
                started(w_ref.at[0, 2 * width :, columns], w_buf.at[width:, columns]),
                started(acc_ref.at[:, columns], acc.at[:, columns]),
            ]
        strips.append(strip)
    last = started(down_ref.at[0], w_down)
    for copy in inputs:
        copy.wait()
    x = x_buf[...]
    for step, strip in enumerate(strips):
        for copy in strip:
            copy.wait()
        at = step * tile
        gate = acc[:, at : at + tile] + jnp.dot(
            x, w_buf[:, at : at + tile], preferred_element_type=F32
        )
        up = acc[:, ff + at : ff + at + tile] + jnp.dot(
            x, w_buf[:, ff + at : ff + at + tile], preferred_element_type=F32
        )
        hidden[:, at : at + tile] = (jax.nn.silu(gate) * up).astype(BF16)
    last.wait()
    width = out_kept.shape[1]
    mine = pl.multiple_of(side * width, width)
    other = pl.multiple_of((1 - side) * width, width)

    def projected(columns):
        return jnp.dot(hidden[...], w_down[:, columns], preferred_element_type=F32).astype(BF16)

    out_handed[...] = projected(pl.ds(other, width))
    back = [started(out_handed, handed_ref)]
    out_direct[...] = projected(pl.ds(2 * width, out_direct.shape[1]))
    back.append(started(out_direct, direct_ref))
    out_kept[...] = projected(pl.ds(mine, width))
    back.append(started(out_kept, kept_ref))
    for copy in back:
        copy.wait()


def attention_body(
    rows_ref,
    gain_ref,
    near_ref,
    across_ref,
    other_near_ref,
    other_across_ref,
    qg_ref,
    kg_ref,
    cos_ref,
    sin_ref,
    handed_ref,
    kept_ref,
    direct_ref,
    w_ref,
):
    side = lax.axis_index("tp") % 2
    place = lax.axis_index("ep")
    along, core = place // 16, place % 2
    sources = (
        (near_ref, along, core),
        (across_ref, 1 - along, core),
        (other_near_ref, along, 1 - core),
        (other_across_ref, 1 - along, 1 - core),
    )
    block = w_ref.shape[0] // 32
    for ref, x_at, core_at in sources:
        for z in range(8):
            start = pl.multiple_of(((x_at * 8 + z) * 2 + core_at) * block, block)
            w_ref[pl.ds(start, block), :] = ref[z * block : (z + 1) * block, :]
    seq = rows_ref.shape[0]
    heads = (w_ref.shape[1] // HD - 2) // 2
    wide = rows_ref[...].astype(F32)
    normed = (wide * inverse_rms(wide) * gain_ref[...]).astype(BF16)
    columns = (heads + 2) * HD
    qkv = jnp.dot(normed, w_ref[:, :columns], preferred_element_type=F32)
    cosine, sine = cos_ref[...], sin_ref[...]

    def turned(values, gain):
        values = values * inverse_rms(values) * gain
        return (values * cosine + pltpu.roll(values, HD // 2, 1) * sine).astype(BF16)

    keys = turned(qkv[:, heads * HD : (heads + 1) * HD], kg_ref[...])
    values = qkv[:, (heads + 1) * HD :].astype(BF16)
    below = lax.broadcasted_iota(jnp.int32, (seq, seq), 0)
    above = lax.broadcasted_iota(jnp.int32, (seq, seq), 1)
    causal = below >= above
    parts = []
    for head in range(heads):
        query = turned(qkv[:, head * HD : (head + 1) * HD], qg_ref[...])
        logits = lax.dot_general(query, keys, NT, preferred_element_type=F32) * HD**-0.5
        logits = jnp.where(causal, logits, -1e30)
        expo = jnp.exp(logits - jnp.max(logits, -1, keepdims=True))
        probs = (expo / jnp.sum(expo, -1, keepdims=True)).astype(BF16)
        parts.append(jnp.dot(probs, values, preferred_element_type=F32).astype(BF16))
    attended = jnp.concatenate(parts, 1)
    width = kept_ref.shape[1]
    mine = pl.multiple_of(side * width, width)
    other = pl.multiple_of((1 - side) * width, width)
    handed_ref[...] = lax.dot_general(
        attended, w_ref[pl.ds(other, width), columns:], NT, preferred_element_type=F32
    ).astype(BF16)
    kept_ref[...] = lax.dot_general(
        attended, w_ref[pl.ds(mine, width), columns:], NT, preferred_element_type=F32
    )
    direct_ref[...] = lax.dot_general(
        attended, w_ref[2 * width :, columns:], NT, preferred_element_type=F32
    )


def combine_body(map_ref, shared_ref, both_ref, kept_ref, got_ref, direct_ref, out_ref):
    width = kept_ref.shape[1]
    shared = jnp.dot(map_ref[...], shared_ref[...], preferred_element_type=F32)
    out_ref[:, :width] = (shared + kept_ref[...] + got_ref[...].astype(F32)).astype(BF16)
    both = jnp.dot(map_ref[...], both_ref[...], preferred_element_type=F32)
    out_ref[:, width:] = (both + direct_ref[...]).astype(BF16)


def local(
    residual_in,
    shortcut,
    attn_gain,
    moe_gain,
    query_weight,
    key_value,
    output_weight,
    query_gain,
    key_gain,
    router_weight,
    expert_ids,
    gate_up_weight,
    down_weight,
):
    n_ep = lax.axis_size("ep")
    n_tp = lax.axis_size("tp")
    rank = lax.axis_index("tp")
    rows, d_model = residual_in.shape
    direct_in = d_model // 8
    shared_in = (d_model - direct_in) // 2
    direct = d_model // 4
    shared = (d_model - direct) // 2
    places = n_ep * SLOTS
    ff2 = gate_up_weight.shape[2]
    ff = ff2 // 2
    qh_dev = query_weight.shape[1] // HD
    kv_head = rank * qh_dev // (QH // KVH)
    along_z = [[x * 16 + z * 2 + c for z in range(8)] for x in range(2) for c in range(2)]
    partner = [(i, i ^ 1) for i in range(n_tp)]

    own_key = lax.dynamic_slice_in_dim(key_value, kv_head * HD, HD, 1)
    own_value = lax.dynamic_slice_in_dim(key_value, (KVH + kv_head) * HD, HD, 1)
    packed = jnp.concatenate([query_weight, own_key, own_value, output_weight], 1)
    near = lax.all_gather(packed, "ep", axis=0, tiled=True, axis_index_groups=along_z)

    def to_owners(value):
        return lax.all_to_all(value, "ep", split_axis=0, concat_axis=0, tiled=True)

    def swapped(value):
        return lax.ppermute(value, "tp", partner)

    moe_gain = moe_gain[None, :]
    ids = expert_ids.T
    outgoing, outgoing_both = call(
        dispatch_body,
        [
            jax.ShapeDtypeStruct((places, shared_in), BF16),
            jax.ShapeDtypeStruct((places, direct_in), BF16),
        ],
        (shortcut, moe_gain, ids),
        2 * places * rows * (shared_in + direct_in),
    )
    arrived = to_owners(outgoing)
    received = swapped(arrived)
    arrived_both = to_owners(outgoing_both)
    (combine,) = call(
        combine_map_body,
        [jax.ShapeDtypeStruct((rows, places), BF16)],
        (shortcut, moe_gain, router_weight, ids),
        2 * rows * 128 * d_model,
        cost=0,
    )
    (acc,) = call(
        first_part_body,
        [jax.ShapeDtypeStruct((places, ff2), F32)],
        (arrived, gate_up_weight),
        2 * places * shared_in * ff2,
        specs=[vmem(), anywhere()],
        scratch=[pltpu.VMEM((shared_in, ff2), BF16), pltpu.SemaphoreType.DMA],
    )
    out_both, handed, kept = call(
        expert_body,
        [
            jax.ShapeDtypeStruct((places, direct), BF16),
            jax.ShapeDtypeStruct((places, shared), BF16),
            jax.ShapeDtypeStruct((places, shared), BF16),
        ],
        (acc, received, arrived_both, gate_up_weight, down_weight, near),
        2 * places * (shared_in + direct_in) * ff2 + 2 * places * ff * d_model,
        specs=[anywhere()] * 6,
        out_specs=[anywhere()] * 3,
        scratch=[
            pltpu.VMEM((places, ff2), F32),
            pltpu.VMEM((places, shared_in + direct_in), BF16),
            pltpu.VMEM((shared_in + direct_in, ff2), BF16),
            pltpu.VMEM((ff, d_model), BF16),
            pltpu.VMEM((places, ff), BF16),
            pltpu.VMEM((places, direct), BF16),
            pltpu.VMEM((places, shared), BF16),
            pltpu.VMEM((places, shared), BF16),
            pltpu.SemaphoreType.DMA((32,)),
        ],
    )
    across = lax.ppermute(near, "ep", [(i, i ^ 16) for i in range(n_ep)])
    cores = [(i, i ^ 1) for i in range(n_ep)]
    other_near = lax.ppermute(near, "ep", cores)
    got = swapped(handed)
    returned_both = to_owners(out_both)
    expert_out = (kept.astype(F32) + got.astype(F32)).astype(BF16)
    returned = to_owners(expert_out)
    (across,) = call(
        relay_body,
        [jax.ShapeDtypeStruct(across.shape, BF16)],
        (across, expert_out),
        0,
        cost=0,
        limit=1,
        specs=[anywhere()] * 2,
        out_specs=[anywhere()],
        aliases={0: 0},
    )
    other_across = lax.ppermute(across, "ep", cores)

    position = jnp.arange(rows, dtype=F32)
    freq = ROPE_BASE ** (-jnp.arange(HD // 2, dtype=F32) * 2.0 / HD)
    angle = position[:, None] * freq[None, :]
    cosine, sine = jnp.cos(angle), jnp.sin(angle)
    cosine = jnp.concatenate([cosine, cosine], 1)
    sine = jnp.concatenate([-sine, sine], 1)
    att_handed, att_kept, att_both = call(
        attention_body,
        [
            jax.ShapeDtypeStruct((rows, shared), BF16),
            jax.ShapeDtypeStruct((rows, shared), F32),
            jax.ShapeDtypeStruct((rows, direct), F32),
        ],
        (
            residual_in,
            attn_gain[None, :],
            near,
            across,
            other_near,
            other_across,
            query_gain[None, :],
            key_gain[None, :],
            cosine,
            sine,
        ),
        2 * rows * d_model * packed.shape[1],
        cost=0,
        scratch=[pltpu.VMEM((d_model, packed.shape[1]), BF16)],
    )
    att_got = swapped(att_handed)
    (total,) = call(
        combine_body,
        [jax.ShapeDtypeStruct((rows, shared + direct), BF16)],
        (combine, returned, returned_both, att_kept, att_got, att_both),
        2 * rows * places * (shared + direct),
        limit=16,
    )
    share = rows // n_tp
    terms = lax.all_to_all(
        total.reshape(n_tp, share, shared + direct),
        "tp",
        split_axis=0,
        concat_axis=0,
        tiled=True,
    )
    terms = terms.astype(F32)
    sums = [jnp.sum(terms[h::2, :, :shared], 0) for h in range(2)]
    sums = jnp.concatenate(sums + [jnp.sum(terms[:, :, shared:], 0)], 1)
    own = lax.dynamic_slice_in_dim(residual_in, rank * share, share, 0)
    mine = (own.astype(F32) + sums).astype(BF16)
    everyone = lax.all_to_all(
        jnp.broadcast_to(mine[None], (n_tp, share, d_model)),
        "tp",
        split_axis=0,
        concat_axis=0,
        tiled=True,
    )
    return everyone.reshape(rows, d_model)


def solution(mesh):
    return jax.shard_map(
        local,
        mesh=mesh,
        in_specs=(
            P("ep", None),
            P("ep", None),
            P(),
            P(),
            P("ep", "tp"),
            P("ep", None),
            P("ep", "tp"),
            P(),
            P(),
            P(),
            P("ep", None),
            P(("ep", "tp"), None, None),
            P(("ep", "tp"), None, None),
        ),
        out_specs=P("ep", None),
        check_vma=False,
    )
```

```python
import functools

import jax
import jax.numpy as jnp
from jax import lax
from jax.experimental import pallas as pl
from jax.experimental.pallas import tpu as pltpu
from jax.sharding import PartitionSpec as P

HD = 128
QH = 32
KVH = 4
TOPK = 8
SLOTS = 16

EPS = 1e-06
ROPE_BASE = 1000000.0
F32 = jnp.float32
BF16 = jnp.bfloat16
NT = (((1,), (1,)), ((), ()))


def vmem():
    return pl.BlockSpec(memory_space=pltpu.VMEM)


def anywhere():
    return pl.BlockSpec(memory_space=pl.ANY)


def call(body, out_shape, args, flops, extra_bytes=0, scratch=(), specs=None, out_specs=None, aliases=None, cost=None, limit=56):
    moved = extra_bytes + sum(a.size * a.dtype.itemsize for a in args)
    moved += sum(o.size * o.dtype.itemsize for o in out_shape)
    return pl.pallas_call(
        body,
        out_shape=out_shape,
        in_specs=specs or [vmem()] * len(args),
        out_specs=out_specs or [vmem()] * len(out_shape),
        scratch_shapes=list(scratch),
        input_output_aliases=aliases or {},
        compiler_params=pltpu.CompilerParams(vmem_limit_bytes=limit * 1024 * 1024),
        cost_estimate=pl.CostEstimate(
            flops=flops if cost is None else cost,
            bytes_accessed=moved if cost is None else cost,
            transcendentals=0,
        ),
    )(*args)


def inverse_rms(wide):
    return lax.rsqrt(jnp.mean(wide * wide, -1, keepdims=True) + EPS)


def slots_of(ids_ref, experts):
    rows = ids_ref.shape[1]
    expert = lax.broadcasted_iota(jnp.int32, (experts, rows), 0)
    hit = ids_ref[0:1, :] == expert
    for k in range(1, TOPK):
        hit = hit | (ids_ref[k : k + 1, :] == expert)
    before = lax.broadcasted_iota(jnp.int32, (rows, rows), 0)
    after = lax.broadcasted_iota(jnp.int32, (rows, rows), 1)
    upper = jnp.where(before < after, 1.0, 0.0).astype(BF16)
    earlier = jnp.dot(jnp.where(hit, 1.0, 0.0).astype(BF16), upper, preferred_element_type=F32)
    slot = jnp.where(hit, earlier, -1.0).astype(BF16)
    places = experts // 4 * SLOTS
    place = lax.broadcasted_iota(jnp.int32, (places, experts), 0)
    column = lax.broadcasted_iota(jnp.int32, (places, experts), 1)
    group = lax.axis_index("tp") // 2
    pick = jnp.where(column == place // SLOTS * 4 + group, 1.0, 0.0).astype(BF16)
    spread = jnp.dot(pick, slot, preferred_element_type=F32)
    wanted = lax.broadcasted_iota(jnp.int32, spread.shape, 0) % SLOTS
    return hit, pick, spread == wanted.astype(F32)


def dispatch_body(rows_ref, gain_ref, ids_ref, shared_ref, direct_ref):
    side = lax.axis_index("tp") % 2
    places, width = shared_ref.shape
    _, _, filled = slots_of(ids_ref, places // SLOTS * 4)
    chosen = jnp.where(filled, 1.0, 0.0).astype(BF16)
    scale = inverse_rms(rows_ref[...].astype(F32))

    def place_columns(columns, out_ref):
        part = rows_ref[:, columns].astype(F32)
        normed = (part * scale * gain_ref[:, columns]).astype(BF16)
        out_ref[...] = jnp.dot(chosen, normed, preferred_element_type=F32).astype(BF16)

    place_columns(pl.ds(pl.multiple_of(side * width, width), width), shared_ref)
    place_columns(pl.ds(2 * width, direct_ref.shape[1]), direct_ref)


def combine_map_body(rows_ref, gain_ref, router_ref, ids_ref, out_ref):
    hit, pick, filled = slots_of(ids_ref, router_ref.shape[0])
    wide = rows_ref[...].astype(F32)
    normed = (wide * inverse_rms(wide) * gain_ref[...]).astype(BF16)
    logits = lax.dot_general(router_ref[...], normed, NT, preferred_element_type=F32)
    scores = jnp.where(hit, jax.nn.sigmoid(logits), 0.0)
    gates = (scores / jnp.sum(scores, 0, keepdims=True)).astype(BF16)
    gate = jnp.dot(pick, gates, preferred_element_type=F32)
    out_ref[...] = jnp.where(filled, gate, 0.0).T.astype(BF16)


def relay_body(value_ref, after_ref, out_ref):
    pass


def first_part_body(own_ref, w_ref, out_ref, w_buf, sem):
    width = own_ref.shape[1]
    mine = pl.multiple_of(lax.axis_index("tp") % 2 * width, width)
    copy = pltpu.make_async_copy(w_ref.at[0, pl.ds(mine, width)], w_buf, sem)
    copy.start()
    copy.wait()
    out_ref[...] = jnp.dot(own_ref[...], w_buf[...], preferred_element_type=F32)


def expert_body(
    acc_ref,
    got_ref,
    both_ref,
    w_ref,
    down_ref,
    near_ref,
    direct_ref,
    handed_ref,
    hidden_ref,
    acc,
    w_buf,
    w_down,
    hidden,
    out_direct,
    out_handed,
    sems,
):
    side = lax.axis_index("tp") % 2
    used = iter(range(32))

    def started(source, target):
        copy = pltpu.make_async_copy(source, target, sems.at[next(used)])
        copy.start()
        return copy

    width = got_ref.shape[1]
    other = pl.multiple_of((1 - side) * width, width)
    ff = hidden.shape[1]
    tile = 256
    split = width
    strips = []
    for at in range(0, ff, tile):
        strip = []
        for start in (at, ff + at):
            columns = pl.ds(start, tile)
            strip += [
                started(w_ref.at[0, pl.ds(other, width), columns], w_buf.at[:width, columns]),
                started(w_ref.at[0, 2 * width :, columns], w_buf.at[width:, columns]),
                started(acc_ref.at[:, columns], acc.at[:, columns]),
            ]
        strips.append(strip)
    width = out_handed.shape[1]
    partner = pl.multiple_of((1 - side) * width, width)
    last = [
        started(down_ref.at[0, :, pl.ds(partner, width)], w_down.at[:, :width]),
        started(down_ref.at[0, :, 2 * width :], w_down.at[:, width:]),
    ]

    def product(columns):
        got = jnp.dot(got_ref[...], w_buf[:split, columns], preferred_element_type=F32)
        both = jnp.dot(both_ref[...], w_buf[split:, columns], preferred_element_type=F32)
        return acc[:, columns] + got + both

    for step, strip in enumerate(strips):
        for copy in strip:
            copy.wait()
        at = step * tile
        gate = product(slice(at, at + tile))
        up = product(slice(ff + at, ff + at + tile))
        hidden[:, at : at + tile] = (jax.nn.silu(gate) * up).astype(BF16)
    back = [started(hidden, hidden_ref)]
    for copy in last:
        copy.wait()

    def projected(columns):
        return jnp.dot(hidden[...], w_down[:, columns], preferred_element_type=F32).astype(BF16)

    width = out_handed.shape[1]
    out_handed[...] = projected(pl.ds(0, width))
    back.append(started(out_handed, handed_ref))
    out_direct[...] = projected(pl.ds(width, out_direct.shape[1]))
    back.append(started(out_direct, direct_ref))
    for copy in back:
        copy.wait()


def kept_body(hidden_ref, down_ref, out_ref, w_down, sem):
    width = out_ref.shape[1]
    mine = pl.multiple_of(lax.axis_index("tp") % 2 * width, width)
    copy = pltpu.make_async_copy(down_ref.at[0, :, pl.ds(mine, width)], w_down, sem)
    copy.start()
    copy.wait()
    out_ref[...] = jnp.dot(
        hidden_ref[...], w_down[...], preferred_element_type=F32
    ).astype(BF16)


def attention_body(
    rows_ref,
    gain_ref,
    near_ref,
    across_ref,
    other_near_ref,
    other_across_ref,
    qg_ref,
    kg_ref,
    cos_ref,
    sin_ref,
    handed_ref,
    kept_ref,
    direct_ref,
    w_ref,
):
    side = lax.axis_index("tp") % 2
    place = lax.axis_index("ep")
    along, core = place // 16, place % 2
    sources = (
        (near_ref, along, core),
        (across_ref, 1 - along, core),
        (other_near_ref, along, 1 - core),
        (other_across_ref, 1 - along, 1 - core),
    )
    block = w_ref.shape[0] // 32
    for ref, x_at, core_at in sources:
        for z in range(8):
            start = pl.multiple_of(((x_at * 8 + z) * 2 + core_at) * block, block)
            w_ref[pl.ds(start, block), :] = ref[z * block : (z + 1) * block, :]
    seq = rows_ref.shape[0]
    heads = (w_ref.shape[1] // HD - 2) // 2
    wide = rows_ref[...].astype(F32)
    normed = (wide * inverse_rms(wide) * gain_ref[...]).astype(BF16)
    columns = (heads + 2) * HD
    qkv = jnp.dot(normed, w_ref[:, :columns], preferred_element_type=F32)
    cosine, sine = cos_ref[...], sin_ref[...]

    def turned(values, gain):
        values = values * inverse_rms(values) * gain
        return (values * cosine + pltpu.roll(values, HD // 2, 1) * sine).astype(BF16)

    keys = turned(qkv[:, heads * HD : (heads + 1) * HD], kg_ref[...])
    values = qkv[:, (heads + 1) * HD :].astype(BF16)
    below = lax.broadcasted_iota(jnp.int32, (seq, seq), 0)
    above = lax.broadcasted_iota(jnp.int32, (seq, seq), 1)
    causal = below >= above
    parts = []
    for head in range(heads):
        query = turned(qkv[:, head * HD : (head + 1) * HD], qg_ref[...])
        logits = lax.dot_general(query, keys, NT, preferred_element_type=F32) * HD**-0.5
        logits = jnp.where(causal, logits, -1e30)
        expo = jnp.exp(logits - jnp.max(logits, -1, keepdims=True))
        probs = (expo / jnp.sum(expo, -1, keepdims=True)).astype(BF16)
        parts.append(jnp.dot(probs, values, preferred_element_type=F32).astype(BF16))
    attended = jnp.concatenate(parts, 1)
    width = kept_ref.shape[1]
    mine = pl.multiple_of(side * width, width)
    other = pl.multiple_of((1 - side) * width, width)
    handed_ref[...] = lax.dot_general(
        attended, w_ref[pl.ds(other, width), columns:], NT, preferred_element_type=F32
    ).astype(BF16)
    kept_ref[...] = lax.dot_general(
        attended, w_ref[pl.ds(mine, width), columns:], NT, preferred_element_type=F32
    )
    direct_ref[...] = lax.dot_general(
        attended, w_ref[2 * width :, columns:], NT, preferred_element_type=F32
    )


def combine_body(
    map_ref, shared_ref, both_ref, kept_ref, got_ref, direct_ref, own_ref, out_ref, own_out_ref
):
    width = kept_ref.shape[1]
    shared = jnp.dot(map_ref[...], shared_ref[...], preferred_element_type=F32)
    out_ref[:, :width] = (shared + kept_ref[...] + got_ref[...].astype(F32)).astype(BF16)
    both = jnp.dot(map_ref[...], both_ref[...], preferred_element_type=F32)
    out_ref[:, width:] = (both + direct_ref[...]).astype(BF16)


def local(
    residual_in,
    shortcut,
    attn_gain,
    moe_gain,
    query_weight,
    key_value,
    output_weight,
    query_gain,
    key_gain,
    router_weight,
    expert_ids,
    gate_up_weight,
    down_weight,
):
    n_ep = lax.axis_size("ep")
    n_tp = lax.axis_size("tp")
    rank = lax.axis_index("tp")
    rows, d_model = residual_in.shape
    direct_in = d_model // 8
    shared_in = (d_model - direct_in) // 2
    direct = d_model // 4
    shared = (d_model - direct) // 2
    places = n_ep * SLOTS
    ff2 = gate_up_weight.shape[2]
    ff = ff2 // 2
    qh_dev = query_weight.shape[1] // HD
    kv_head = rank * qh_dev // (QH // KVH)
    along_z = [[x * 16 + z * 2 + c for z in range(8)] for x in range(2) for c in range(2)]
    partner = [(i, i ^ 1) for i in range(n_tp)]

    own_key = lax.dynamic_slice_in_dim(key_value, kv_head * HD, HD, 1)
    own_value = lax.dynamic_slice_in_dim(key_value, (KVH + kv_head) * HD, HD, 1)
    packed = jnp.concatenate([query_weight, own_key, own_value, output_weight], 1)
    near = lax.all_gather(packed, "ep", axis=0, tiled=True, axis_index_groups=along_z)

    def to_owners(value):
        return lax.all_to_all(value, "ep", split_axis=0, concat_axis=0, tiled=True)

    def swapped(value):
        return lax.ppermute(value, "tp", partner)

    moe_gain = moe_gain[None, :]
    ids = expert_ids.T
    outgoing, outgoing_both = call(
        dispatch_body,
        [
            jax.ShapeDtypeStruct((places, shared_in), BF16),
            jax.ShapeDtypeStruct((places, direct_in), BF16),
        ],
        (shortcut, moe_gain, ids),
        2 * places * rows * (shared_in + direct_in),
    )
    arrived = to_owners(outgoing)
    received = swapped(arrived)
    arrived_both = to_owners(outgoing_both)
    (combine,) = call(
        combine_map_body,
        [jax.ShapeDtypeStruct((rows, places), BF16)],
        (shortcut, moe_gain, router_weight, ids),
        2 * rows * 128 * d_model,
        cost=0,
    )
    (acc,) = call(
        first_part_body,
        [jax.ShapeDtypeStruct((places, ff2), F32)],
        (arrived, gate_up_weight),
        2 * places * shared_in * ff2,
        specs=[vmem(), anywhere()],
        scratch=[pltpu.VMEM((shared_in, ff2), BF16), pltpu.SemaphoreType.DMA],
    )
    out_both, handed, hidden = call(
        expert_body,
        [
            jax.ShapeDtypeStruct((places, direct), BF16),
            jax.ShapeDtypeStruct((places, shared), BF16),
            jax.ShapeDtypeStruct((places, ff), BF16),
        ],
        (acc, received, arrived_both, gate_up_weight, down_weight, near),
        2 * places * (shared_in + direct_in) * ff2 + 2 * places * ff * d_model,
        limit=52,
        specs=[anywhere(), vmem(), vmem()] + [anywhere()] * 3,
        out_specs=[anywhere()] * 3,
        scratch=[
            pltpu.VMEM((places, ff2), F32),
            pltpu.VMEM((shared_in + direct_in, ff2), BF16),
            pltpu.VMEM((ff, shared + direct), BF16),
            pltpu.VMEM((places, ff), BF16),
            pltpu.VMEM((places, direct), BF16),
            pltpu.VMEM((places, shared), BF16),
            pltpu.SemaphoreType.DMA((32,)),
        ],
    )
    (kept,) = call(
        kept_body,
        [jax.ShapeDtypeStruct((places, shared), BF16)],
        (hidden, down_weight),
        0,
        cost=0,
        specs=[vmem(), anywhere()],
        scratch=[pltpu.VMEM((ff, shared), BF16), pltpu.SemaphoreType.DMA],
    )
    across = lax.ppermute(near, "ep", [(i, i ^ 16) for i in range(n_ep)])
    cores = [(i, i ^ 1) for i in range(n_ep)]
    other_near = lax.ppermute(near, "ep", cores)
    got = swapped(handed)
    returned_both = to_owners(out_both)
    expert_out = (kept.astype(F32) + got.astype(F32)).astype(BF16)
    returned = to_owners(expert_out)
    (across,) = call(
        relay_body,
        [jax.ShapeDtypeStruct(across.shape, BF16)],
        (across, expert_out),
        0,
        cost=0,
        limit=1,
        specs=[anywhere()] * 2,
        out_specs=[anywhere()],
        aliases={0: 0},
    )
    other_across = lax.ppermute(across, "ep", cores)

    position = jnp.arange(rows, dtype=F32)
    freq = ROPE_BASE ** (-jnp.arange(HD // 2, dtype=F32) * 2.0 / HD)
    angle = position[:, None] * freq[None, :]
    cosine, sine = jnp.cos(angle), jnp.sin(angle)
    cosine = jnp.concatenate([cosine, cosine], 1)
    sine = jnp.concatenate([-sine, sine], 1)
    att_handed, att_kept, att_both = call(
        attention_body,
        [
            jax.ShapeDtypeStruct((rows, shared), BF16),
            jax.ShapeDtypeStruct((rows, shared), F32),
            jax.ShapeDtypeStruct((rows, direct), F32),
        ],
        (
            residual_in,
            attn_gain[None, :],
            near,
            across,
            other_near,
            other_across,
            query_gain[None, :],
            key_gain[None, :],
            cosine,
            sine,
        ),
        2 * rows * d_model * packed.shape[1],
        cost=0,
        scratch=[pltpu.VMEM((d_model, packed.shape[1]), BF16)],
    )
    att_got = swapped(att_handed)
    share = rows // n_tp
    own = lax.dynamic_slice_in_dim(residual_in, rank * share, share, 0)
    total, own = call(
        combine_body,
        [
            jax.ShapeDtypeStruct((rows, shared + direct), BF16),
            jax.ShapeDtypeStruct(own.shape, BF16),
        ],
        (combine, returned, returned_both, att_kept, att_got, att_both, own),
        2 * rows * places * (shared + direct),
        limit=16,
        specs=[vmem()] * 6 + [anywhere()],
        out_specs=[vmem(), anywhere()],
        aliases={6: 1},
    )
    terms = lax.all_to_all(
        total.reshape(n_tp, share, shared + direct),
        "tp",
        split_axis=0,
        concat_axis=0,
        tiled=True,
    )
    terms = terms.astype(F32)
    sums = [jnp.sum(terms[h::2, :, :shared], 0) for h in range(2)]
    sums = jnp.concatenate(sums + [jnp.sum(terms[:, :, shared:], 0)], 1)
    mine = (own.astype(F32) + sums).astype(BF16)
    everyone = lax.all_to_all(
        jnp.broadcast_to(mine[None], (n_tp, share, d_model)),
        "tp",
        split_axis=0,
        concat_axis=0,
        tiled=True,
    )
    return everyone.reshape(rows, d_model)


def solution(mesh):
    return jax.shard_map(
        local,
        mesh=mesh,
        in_specs=(
            P("ep", None),
            P("ep", None),
            P(),
            P(),
            P("ep", "tp"),
            P("ep", None),
            P("ep", "tp"),
            P(),
            P(),
            P(),
            P("ep", None),
            P(("ep", "tp"), None, None),
            P(("ep", "tp"), None, None),
        ),
        out_specs=P("ep", None),
        check_vma=False,
    )
```

```python
import functools

import jax
import jax.numpy as jnp
from jax import lax
from jax.experimental import pallas as pl
from jax.experimental.pallas import tpu as pltpu
from jax.sharding import PartitionSpec as P

HD = 128
QH = 32
KVH = 4
TOPK = 8
SLOTS = 16

EPS = 1e-06
ROPE_BASE = 1000000.0
F32 = jnp.float32
BF16 = jnp.bfloat16
NT = (((1,), (1,)), ((), ()))


def vmem():
    return pl.BlockSpec(memory_space=pltpu.VMEM)


def anywhere():
    return pl.BlockSpec(memory_space=pl.ANY)


def call(body, out_shape, args, flops, extra_bytes=0, scratch=(), specs=None, out_specs=None, aliases=None, cost=None, limit=56):
    moved = extra_bytes + sum(a.size * a.dtype.itemsize for a in args)
    moved += sum(o.size * o.dtype.itemsize for o in out_shape)
    return pl.pallas_call(
        body,
        out_shape=out_shape,
        in_specs=specs or [vmem()] * len(args),
        out_specs=out_specs or [vmem()] * len(out_shape),
        scratch_shapes=list(scratch),
        input_output_aliases=aliases or {},
        compiler_params=pltpu.CompilerParams(vmem_limit_bytes=limit * 1024 * 1024),
        cost_estimate=pl.CostEstimate(
            flops=flops if cost is None else cost,
            bytes_accessed=moved if cost is None else cost,
            transcendentals=0,
        ),
    )(*args)


def inverse_rms(wide):
    return lax.rsqrt(jnp.mean(wide * wide, -1, keepdims=True) + EPS)


def slots_of(ids_ref, experts):
    rows = ids_ref.shape[1]
    expert = lax.broadcasted_iota(jnp.int32, (experts, rows), 0)
    hit = ids_ref[0:1, :] == expert
    for k in range(1, TOPK):
        hit = hit | (ids_ref[k : k + 1, :] == expert)
    before = lax.broadcasted_iota(jnp.int32, (rows, rows), 0)
    after = lax.broadcasted_iota(jnp.int32, (rows, rows), 1)
    upper = jnp.where(before < after, 1.0, 0.0).astype(BF16)
    earlier = jnp.dot(jnp.where(hit, 1.0, 0.0).astype(BF16), upper, preferred_element_type=F32)
    slot = jnp.where(hit, earlier, -1.0).astype(BF16)
    places = experts // 4 * SLOTS
    place = lax.broadcasted_iota(jnp.int32, (places, experts), 0)
    column = lax.broadcasted_iota(jnp.int32, (places, experts), 1)
    group = lax.axis_index("tp") // 2
    pick = jnp.where(column == place // SLOTS * 4 + group, 1.0, 0.0).astype(BF16)
    spread = jnp.dot(pick, slot, preferred_element_type=F32)
    wanted = lax.broadcasted_iota(jnp.int32, spread.shape, 0) % SLOTS
    return hit, pick, spread == wanted.astype(F32)


def dispatch_body(rows_ref, gain_ref, ids_ref, shared_ref, direct_ref):
    side = lax.axis_index("tp") % 2
    places, width = shared_ref.shape
    _, _, filled = slots_of(ids_ref, places // SLOTS * 4)
    chosen = jnp.where(filled, 1.0, 0.0).astype(BF16)
    scale = inverse_rms(rows_ref[...].astype(F32))

    def place_columns(columns, out_ref):
        part = rows_ref[:, columns].astype(F32)
        normed = (part * scale * gain_ref[:, columns]).astype(BF16)
        out_ref[...] = jnp.dot(chosen, normed, preferred_element_type=F32).astype(BF16)

    place_columns(pl.ds(pl.multiple_of(side * width, width), width), shared_ref)
    place_columns(pl.ds(2 * width, direct_ref.shape[1]), direct_ref)


def combine_map_body(rows_ref, gain_ref, router_ref, ids_ref, out_ref):
    hit, pick, filled = slots_of(ids_ref, router_ref.shape[0])
    wide = rows_ref[...].astype(F32)
    normed = (wide * inverse_rms(wide) * gain_ref[...]).astype(BF16)
    logits = lax.dot_general(router_ref[...], normed, NT, preferred_element_type=F32)
    scores = jnp.where(hit, jax.nn.sigmoid(logits), 0.0)
    gates = (scores / jnp.sum(scores, 0, keepdims=True)).astype(BF16)
    gate = jnp.dot(pick, gates, preferred_element_type=F32)
    out_ref[...] = jnp.where(filled, gate, 0.0).T.astype(BF16)


def relay_body(value_ref, after_ref, out_ref):
    pass


def first_part_body(own_ref, w_ref, out_ref, w_buf, sem):
    width = own_ref.shape[1]
    mine = pl.multiple_of(lax.axis_index("tp") % 2 * width, width)
    copy = pltpu.make_async_copy(w_ref.at[0, pl.ds(mine, width)], w_buf, sem)
    copy.start()
    copy.wait()
    out_ref[...] = jnp.dot(own_ref[...], w_buf[...], preferred_element_type=F32)


def expert_body(
    acc_ref,
    got_ref,
    both_ref,
    w_ref,
    down_ref,
    near_ref,
    direct_ref,
    handed_ref,
    hidden_ref,
    acc,
    w_buf,
    w_down,
    hidden,
    out_direct,
    out_handed,
    sems,
):
    side = lax.axis_index("tp") % 2
    used = iter(range(32))

    def started(source, target):
        copy = pltpu.make_async_copy(source, target, sems.at[next(used)])
        copy.start()
        return copy

    width = got_ref.shape[1]
    other = pl.multiple_of((1 - side) * width, width)
    ff = hidden.shape[1]
    tile = 256
    split = width
    strips = []
    for at in range(0, ff, tile):
        strip = []
        for start in (at, ff + at):
            columns = pl.ds(start, tile)
            strip += [
                started(w_ref.at[0, pl.ds(other, width), columns], w_buf.at[:width, columns]),
                started(w_ref.at[0, 2 * width :, columns], w_buf.at[width:, columns]),
                started(acc_ref.at[:, columns], acc.at[:, columns]),
            ]
        strips.append(strip)
    width = out_handed.shape[1]
    partner = pl.multiple_of((1 - side) * width, width)
    last = [
        started(down_ref.at[0, :, pl.ds(partner, width)], w_down.at[:, :width]),
        started(down_ref.at[0, :, 2 * width :], w_down.at[:, width:]),
    ]

    def product(columns):
        got = jnp.dot(got_ref[...], w_buf[:split, columns], preferred_element_type=F32)
        both = jnp.dot(both_ref[...], w_buf[split:, columns], preferred_element_type=F32)
        return acc[:, columns] + got + both

    for step, strip in enumerate(strips):
        for copy in strip:
            copy.wait()
        at = step * tile
        gate = product(slice(at, at + tile))
        up = product(slice(ff + at, ff + at + tile))
        hidden[:, at : at + tile] = (jax.nn.silu(gate) * up).astype(BF16)
    back = [started(hidden, hidden_ref)]
    for copy in last:
        copy.wait()

    def projected(columns):
        return jnp.dot(hidden[...], w_down[:, columns], preferred_element_type=F32).astype(BF16)

    width = out_handed.shape[1]
    out_handed[...] = projected(pl.ds(0, width))
    back.append(started(out_handed, handed_ref))
    out_direct[...] = projected(pl.ds(width, out_direct.shape[1]))
    back.append(started(out_direct, direct_ref))
    for copy in back:
        copy.wait()


def kept_body(hidden_ref, down_ref, out_ref, w_down, sem):
    width = out_ref.shape[1]
    mine = pl.multiple_of(lax.axis_index("tp") % 2 * width, width)
    copy = pltpu.make_async_copy(down_ref.at[0, :, pl.ds(mine, width)], w_down, sem)
    copy.start()
    copy.wait()
    out_ref[...] = jnp.dot(
        hidden_ref[...], w_down[...], preferred_element_type=F32
    ).astype(BF16)


def attention_body(
    rows_ref,
    gain_ref,
    near_ref,
    across_ref,
    other_near_ref,
    other_across_ref,
    qg_ref,
    kg_ref,
    cos_ref,
    sin_ref,
    handed_ref,
    kept_ref,
    direct_ref,
    w_ref,
):
    side = lax.axis_index("tp") % 2
    place = lax.axis_index("ep")
    along, core = place // 16, place % 2
    sources = (
        (near_ref, along, core),
        (across_ref, 1 - along, core),
        (other_near_ref, along, 1 - core),
        (other_across_ref, 1 - along, 1 - core),
    )
    block = w_ref.shape[0] // 32
    for ref, x_at, core_at in sources:
        for z in range(8):
            start = pl.multiple_of(((x_at * 8 + z) * 2 + core_at) * block, block)
            w_ref[pl.ds(start, block), :] = ref[z * block : (z + 1) * block, :]
    seq = rows_ref.shape[0]
    heads = (w_ref.shape[1] // HD - 2) // 2
    wide = rows_ref[...].astype(F32)
    normed = (wide * inverse_rms(wide) * gain_ref[...]).astype(BF16)
    columns = (heads + 2) * HD
    qkv = jnp.dot(normed, w_ref[:, :columns], preferred_element_type=F32)
    cosine, sine = cos_ref[...], sin_ref[...]

    def turned(values, gain):
        values = values * inverse_rms(values) * gain
        return (values * cosine + pltpu.roll(values, HD // 2, 1) * sine).astype(BF16)

    keys = turned(qkv[:, heads * HD : (heads + 1) * HD], kg_ref[...])
    values = qkv[:, (heads + 1) * HD :].astype(BF16)
    below = lax.broadcasted_iota(jnp.int32, (seq, seq), 0)
    above = lax.broadcasted_iota(jnp.int32, (seq, seq), 1)
    causal = below >= above
    parts = []
    for head in range(heads):
        query = turned(qkv[:, head * HD : (head + 1) * HD], qg_ref[...])
        logits = lax.dot_general(query, keys, NT, preferred_element_type=F32) * HD**-0.5
        logits = jnp.where(causal, logits, -1e30)
        expo = jnp.exp(logits - jnp.max(logits, -1, keepdims=True))
        probs = (expo / jnp.sum(expo, -1, keepdims=True)).astype(BF16)
        parts.append(jnp.dot(probs, values, preferred_element_type=F32).astype(BF16))
    attended = jnp.concatenate(parts, 1)
    width = kept_ref.shape[1]
    mine = pl.multiple_of(side * width, width)
    other = pl.multiple_of((1 - side) * width, width)
    handed_ref[...] = lax.dot_general(
        attended, w_ref[pl.ds(other, width), columns:], NT, preferred_element_type=F32
    ).astype(BF16)
    kept_ref[...] = lax.dot_general(
        attended, w_ref[pl.ds(mine, width), columns:], NT, preferred_element_type=F32
    )
    direct_ref[...] = lax.dot_general(
        attended, w_ref[2 * width :, columns:], NT, preferred_element_type=F32
    )


def combine_body(
    map_ref, shared_ref, both_ref, kept_ref, got_ref, direct_ref, own_ref, out_ref, own_out_ref
):
    width = kept_ref.shape[1]
    shared = jnp.dot(map_ref[...], shared_ref[...], preferred_element_type=F32)
    out_ref[:, :width] = (shared + kept_ref[...] + got_ref[...].astype(F32)).astype(BF16)
    both = jnp.dot(map_ref[...], both_ref[...], preferred_element_type=F32)
    out_ref[:, width:] = (both + direct_ref[...]).astype(BF16)


def local(
    residual_in,
    shortcut,
    attn_gain,
    moe_gain,
    query_weight,
    key_value,
    output_weight,
    query_gain,
    key_gain,
    router_weight,
    expert_ids,
    gate_up_weight,
    down_weight,
):
    n_ep = lax.axis_size("ep")
    n_tp = lax.axis_size("tp")
    rank = lax.axis_index("tp")
    rows, d_model = residual_in.shape
    direct_in = d_model // 8
    shared_in = (d_model - direct_in) // 2
    direct = d_model // 4
    shared = (d_model - direct) // 2
    places = n_ep * SLOTS
    ff2 = gate_up_weight.shape[2]
    ff = ff2 // 2
    qh_dev = query_weight.shape[1] // HD
    kv_head = rank * qh_dev // (QH // KVH)
    along_z = [[x * 16 + z * 2 + c for z in range(8)] for x in range(2) for c in range(2)]
    partner = [(i, i ^ 1) for i in range(n_tp)]

    own_key = lax.dynamic_slice_in_dim(key_value, kv_head * HD, HD, 1)
    own_value = lax.dynamic_slice_in_dim(key_value, (KVH + kv_head) * HD, HD, 1)
    packed = jnp.concatenate([query_weight, own_key, own_value, output_weight], 1)
    near = lax.all_gather(packed, "ep", axis=0, tiled=True, axis_index_groups=along_z)

    def to_owners(value):
        return lax.all_to_all(value, "ep", split_axis=0, concat_axis=0, tiled=True)

    def swapped(value):
        return lax.ppermute(value, "tp", partner)

    moe_gain = moe_gain[None, :]
    ids = expert_ids.T
    outgoing, outgoing_both = call(
        dispatch_body,
        [
            jax.ShapeDtypeStruct((places, shared_in), BF16),
            jax.ShapeDtypeStruct((places, direct_in), BF16),
        ],
        (shortcut, moe_gain, ids),
        2 * places * rows * (shared_in + direct_in),
    )
    arrived = to_owners(outgoing)
    received = swapped(arrived)
    arrived_both = to_owners(outgoing_both)
    (combine,) = call(
        combine_map_body,
        [jax.ShapeDtypeStruct((rows, places), BF16)],
        (shortcut, moe_gain, router_weight, ids),
        2 * rows * 128 * d_model,
        cost=0,
        limit=24,
    )
    (acc,) = call(
        first_part_body,
        [jax.ShapeDtypeStruct((places, ff2), F32)],
        (arrived, gate_up_weight),
        2 * places * shared_in * ff2,
        specs=[vmem(), anywhere()],
        scratch=[pltpu.VMEM((shared_in, ff2), BF16), pltpu.SemaphoreType.DMA],
    )
    out_both, handed, hidden = call(
        expert_body,
        [
            jax.ShapeDtypeStruct((places, direct), BF16),
            jax.ShapeDtypeStruct((places, shared), BF16),
            jax.ShapeDtypeStruct((places, ff), BF16),
        ],
        (acc, received, arrived_both, gate_up_weight, down_weight, near),
        2 * places * (shared_in + direct_in) * ff2 + 2 * places * ff * d_model,
        limit=52,
        specs=[anywhere(), vmem(), vmem()] + [anywhere()] * 3,
        out_specs=[anywhere()] * 3,
        scratch=[
            pltpu.VMEM((places, ff2), F32),
            pltpu.VMEM((shared_in + direct_in, ff2), BF16),
            pltpu.VMEM((ff, shared + direct), BF16),
            pltpu.VMEM((places, ff), BF16),
            pltpu.VMEM((places, direct), BF16),
            pltpu.VMEM((places, shared), BF16),
            pltpu.SemaphoreType.DMA((32,)),
        ],
    )
    (kept,) = call(
        kept_body,
        [jax.ShapeDtypeStruct((places, shared), BF16)],
        (hidden, down_weight),
        0,
        cost=0,
        specs=[vmem(), anywhere()],
        scratch=[pltpu.VMEM((ff, shared), BF16), pltpu.SemaphoreType.DMA],
    )
    across = lax.ppermute(near, "ep", [(i, i ^ 16) for i in range(n_ep)])
    cores = [(i, i ^ 1) for i in range(n_ep)]
    other_near = lax.ppermute(near, "ep", cores)
    got = swapped(handed)
    returned_both = to_owners(out_both)
    expert_out = (kept.astype(F32) + got.astype(F32)).astype(BF16)
    returned = to_owners(expert_out)
    (across,) = call(
        relay_body,
        [jax.ShapeDtypeStruct(across.shape, BF16)],
        (across, expert_out),
        0,
        cost=0,
        limit=1,
        specs=[anywhere()] * 2,
        out_specs=[anywhere()],
        aliases={0: 0},
    )
    other_across = lax.ppermute(across, "ep", cores)

    position = jnp.arange(rows, dtype=F32)
    freq = ROPE_BASE ** (-jnp.arange(HD // 2, dtype=F32) * 2.0 / HD)
    angle = position[:, None] * freq[None, :]
    cosine, sine = jnp.cos(angle), jnp.sin(angle)
    cosine = jnp.concatenate([cosine, cosine], 1)
    sine = jnp.concatenate([-sine, sine], 1)
    att_handed, att_kept, att_both = call(
        attention_body,
        [
            jax.ShapeDtypeStruct((rows, shared), BF16),
            jax.ShapeDtypeStruct((rows, shared), F32),
            jax.ShapeDtypeStruct((rows, direct), F32),
        ],
        (
            residual_in,
            attn_gain[None, :],
            near,
            across,
            other_near,
            other_across,
            query_gain[None, :],
            key_gain[None, :],
            cosine,
            sine,
        ),
        2 * rows * d_model * packed.shape[1],
        cost=0,
        scratch=[pltpu.VMEM((d_model, packed.shape[1]), BF16)],
    )
    att_got = swapped(att_handed)
    share = rows // n_tp
    own = lax.dynamic_slice_in_dim(residual_in, rank * share, share, 0)
    total, own = call(
        combine_body,
        [
            jax.ShapeDtypeStruct((rows, shared + direct), BF16),
            jax.ShapeDtypeStruct(own.shape, BF16),
        ],
        (combine, returned, returned_both, att_kept, att_got, att_both, own),
        2 * rows * places * (shared + direct),
        limit=16,
        specs=[vmem()] * 6 + [anywhere()],
        out_specs=[vmem(), anywhere()],
        aliases={6: 1},
    )
    terms = lax.all_to_all(
        total.reshape(n_tp, share, shared + direct),
        "tp",
        split_axis=0,
        concat_axis=0,
        tiled=True,
    )
    terms = terms.astype(F32)
    sums = [jnp.sum(terms[h::2, :, :shared], 0) for h in range(2)]
    sums = jnp.concatenate(sums + [jnp.sum(terms[:, :, shared:], 0)], 1)
    mine = (own.astype(F32) + sums).astype(BF16)
    everyone = lax.all_to_all(
        jnp.broadcast_to(mine[None], (n_tp, share, d_model)),
        "tp",
        split_axis=0,
        concat_axis=0,
        tiled=True,
    )
    return everyone.reshape(rows, d_model)


def solution(mesh):
    return jax.shard_map(
        local,
        mesh=mesh,
        in_specs=(
            P("ep", None),
            P("ep", None),
            P(),
            P(),
            P("ep", "tp"),
            P("ep", None),
            P("ep", "tp"),
            P(),
            P(),
            P(),
            P("ep", None),
            P(("ep", "tp"), None, None),
            P(("ep", "tp"), None, None),
        ),
        out_specs=P("ep", None),
        check_vma=False,
    )
```

```python
import functools

import jax
import jax.numpy as jnp
from jax import lax
from jax.experimental import pallas as pl
from jax.experimental.pallas import tpu as pltpu
from jax.sharding import PartitionSpec as P

HD = 128
QH = 32
KVH = 4
TOPK = 8
SLOTS = 16

EPS = 1e-06
ROPE_BASE = 1000000.0
F32 = jnp.float32
BF16 = jnp.bfloat16
NT = (((1,), (1,)), ((), ()))


def vmem():
    return pl.BlockSpec(memory_space=pltpu.VMEM)


def anywhere():
    return pl.BlockSpec(memory_space=pl.ANY)


def call(body, out_shape, args, flops, extra_bytes=0, scratch=(), specs=None, out_specs=None, aliases=None, cost=None, limit=56):
    moved = extra_bytes + sum(a.size * a.dtype.itemsize for a in args)
    moved += sum(o.size * o.dtype.itemsize for o in out_shape)
    return pl.pallas_call(
        body,
        out_shape=out_shape,
        in_specs=specs or [vmem()] * len(args),
        out_specs=out_specs or [vmem()] * len(out_shape),
        scratch_shapes=list(scratch),
        input_output_aliases=aliases or {},
        compiler_params=pltpu.CompilerParams(vmem_limit_bytes=limit * 1024 * 1024),
        cost_estimate=pl.CostEstimate(
            flops=flops if cost is None else cost,
            bytes_accessed=moved if cost is None else cost,
            transcendentals=0,
        ),
    )(*args)


def inverse_rms(wide):
    return lax.rsqrt(jnp.mean(wide * wide, -1, keepdims=True) + EPS)


def slots_of(ids_ref, experts):
    rows = ids_ref.shape[1]
    expert = lax.broadcasted_iota(jnp.int32, (experts, rows), 0)
    hit = ids_ref[0:1, :] == expert
    for k in range(1, TOPK):
        hit = hit | (ids_ref[k : k + 1, :] == expert)
    before = lax.broadcasted_iota(jnp.int32, (rows, rows), 0)
    after = lax.broadcasted_iota(jnp.int32, (rows, rows), 1)
    upper = jnp.where(before < after, 1.0, 0.0).astype(BF16)
    earlier = jnp.dot(jnp.where(hit, 1.0, 0.0).astype(BF16), upper, preferred_element_type=F32)
    slot = jnp.where(hit, earlier, -1.0).astype(BF16)
    places = experts // 4 * SLOTS
    place = lax.broadcasted_iota(jnp.int32, (places, experts), 0)
    column = lax.broadcasted_iota(jnp.int32, (places, experts), 1)
    group = lax.axis_index("tp") // 2
    pick = jnp.where(column == place // SLOTS * 4 + group, 1.0, 0.0).astype(BF16)
    spread = jnp.dot(pick, slot, preferred_element_type=F32)
    wanted = lax.broadcasted_iota(jnp.int32, spread.shape, 0) % SLOTS
    return hit, pick, spread == wanted.astype(F32)


def dispatch_body(rows_ref, gain_ref, ids_ref, shared_ref, direct_ref):
    side = lax.axis_index("tp") % 2
    places, width = shared_ref.shape
    _, _, filled = slots_of(ids_ref, places // SLOTS * 4)
    chosen = jnp.where(filled, 1.0, 0.0).astype(BF16)
    scale = inverse_rms(rows_ref[...].astype(F32))

    def place_columns(columns, out_ref):
        part = rows_ref[:, columns].astype(F32)
        normed = (part * scale * gain_ref[:, columns]).astype(BF16)
        out_ref[...] = jnp.dot(chosen, normed, preferred_element_type=F32).astype(BF16)

    place_columns(pl.ds(pl.multiple_of(side * width, width), width), shared_ref)
    place_columns(pl.ds(2 * width, direct_ref.shape[1]), direct_ref)


def combine_map_body(rows_ref, gain_ref, router_ref, ids_ref, out_ref):
    hit, pick, filled = slots_of(ids_ref, router_ref.shape[0])
    wide = rows_ref[...].astype(F32)
    normed = (wide * inverse_rms(wide) * gain_ref[...]).astype(BF16)
    logits = lax.dot_general(router_ref[...], normed, NT, preferred_element_type=F32)
    scores = jnp.where(hit, jax.nn.sigmoid(logits), 0.0)
    gates = (scores / jnp.sum(scores, 0, keepdims=True)).astype(BF16)
    gate = jnp.dot(pick, gates, preferred_element_type=F32)
    out_ref[...] = jnp.where(filled, gate, 0.0).T.astype(BF16)


def relay_body(value_ref, after_ref, out_ref):
    pass


def first_part_body(own_ref, w_ref, out_ref, w_buf, sem):
    width = own_ref.shape[1]
    mine = pl.multiple_of(lax.axis_index("tp") % 2 * width, width)
    copy = pltpu.make_async_copy(w_ref.at[0, pl.ds(mine, width)], w_buf, sem)
    copy.start()
    copy.wait()
    out_ref[...] = jnp.dot(
        own_ref[...], w_buf[...], preferred_element_type=F32
    ).astype(BF16)


def expert_body(
    acc_ref,
    got_ref,
    both_ref,
    w_ref,
    down_ref,
    near_ref,
    direct_ref,
    handed_ref,
    hidden_ref,
    acc,
    w_buf,
    w_down,
    hidden,
    out_direct,
    out_handed,
    sems,
):
    side = lax.axis_index("tp") % 2
    used = iter(range(32))

    def started(source, target):
        copy = pltpu.make_async_copy(source, target, sems.at[next(used)])
        copy.start()
        return copy

    width = got_ref.shape[1]
    other = pl.multiple_of((1 - side) * width, width)
    ff = hidden.shape[1]
    tile = 256
    split = width
    strips = []
    for at in range(0, ff, tile):
        strip = []
        for start in (at, ff + at):
            columns = pl.ds(start, tile)
            strip += [
                started(w_ref.at[0, pl.ds(other, width), columns], w_buf.at[:width, columns]),
                started(w_ref.at[0, 2 * width :, columns], w_buf.at[width:, columns]),
                started(acc_ref.at[:, columns], acc.at[:, columns]),
            ]
        strips.append(strip)
    width = out_handed.shape[1]
    partner = pl.multiple_of((1 - side) * width, width)
    last = [
        started(down_ref.at[0, :, pl.ds(partner, width)], w_down.at[:, :width]),
        started(down_ref.at[0, :, 2 * width :], w_down.at[:, width:]),
    ]

    def product(columns):
        got = jnp.dot(got_ref[...], w_buf[:split, columns], preferred_element_type=F32)
        both = jnp.dot(both_ref[...], w_buf[split:, columns], preferred_element_type=F32)
        return acc[:, columns].astype(F32) + got + both

    for step, strip in enumerate(strips):
        for copy in strip:
            copy.wait()
        at = step * tile
        gate = product(slice(at, at + tile))
        up = product(slice(ff + at, ff + at + tile))
        hidden[:, at : at + tile] = (jax.nn.silu(gate) * up).astype(BF16)
    back = [started(hidden, hidden_ref)]
    for copy in last:
        copy.wait()

    def projected(columns):
        return jnp.dot(hidden[...], w_down[:, columns], preferred_element_type=F32).astype(BF16)

    width = out_handed.shape[1]
    out_handed[...] = projected(pl.ds(0, width))
    back.append(started(out_handed, handed_ref))
    out_direct[...] = projected(pl.ds(width, out_direct.shape[1]))
    back.append(started(out_direct, direct_ref))
    for copy in back:
        copy.wait()


def kept_body(hidden_ref, down_ref, out_ref, w_down, sem):
    width = out_ref.shape[1]
    mine = pl.multiple_of(lax.axis_index("tp") % 2 * width, width)
    copy = pltpu.make_async_copy(down_ref.at[0, :, pl.ds(mine, width)], w_down, sem)
    copy.start()
    copy.wait()
    out_ref[...] = jnp.dot(
        hidden_ref[...], w_down[...], preferred_element_type=F32
    ).astype(BF16)


def attention_body(
    rows_ref,
    gain_ref,
    near_ref,
    across_ref,
    other_near_ref,
    other_across_ref,
    qg_ref,
    kg_ref,
    cos_ref,
    sin_ref,
    handed_ref,
    kept_ref,
    direct_ref,
    w_ref,
):
    side = lax.axis_index("tp") % 2
    place = lax.axis_index("ep")
    along, core = place // 16, place % 2
    sources = (
        (near_ref, along, core),
        (across_ref, 1 - along, core),
        (other_near_ref, along, 1 - core),
        (other_across_ref, 1 - along, 1 - core),
    )
    block = w_ref.shape[0] // 32
    for ref, x_at, core_at in sources:
        for z in range(8):
            start = pl.multiple_of(((x_at * 8 + z) * 2 + core_at) * block, block)
            w_ref[pl.ds(start, block), :] = ref[z * block : (z + 1) * block, :]
    seq = rows_ref.shape[0]
    heads = (w_ref.shape[1] // HD - 2) // 2
    wide = rows_ref[...].astype(F32)
    normed = (wide * inverse_rms(wide) * gain_ref[...]).astype(BF16)
    columns = (heads + 2) * HD
    qkv = jnp.dot(normed, w_ref[:, :columns], preferred_element_type=F32)
    cosine, sine = cos_ref[...], sin_ref[...]

    def turned(values, gain):
        values = values * inverse_rms(values) * gain
        return (values * cosine + pltpu.roll(values, HD // 2, 1) * sine).astype(BF16)

    keys = turned(qkv[:, heads * HD : (heads + 1) * HD], kg_ref[...])
    values = qkv[:, (heads + 1) * HD :].astype(BF16)
    below = lax.broadcasted_iota(jnp.int32, (seq, seq), 0)
    above = lax.broadcasted_iota(jnp.int32, (seq, seq), 1)
    causal = below >= above
    parts = []
    for head in range(heads):
        query = turned(qkv[:, head * HD : (head + 1) * HD], qg_ref[...])
        logits = lax.dot_general(query, keys, NT, preferred_element_type=F32) * HD**-0.5
        logits = jnp.where(causal, logits, -1e30)
        expo = jnp.exp(logits - jnp.max(logits, -1, keepdims=True))
        probs = (expo / jnp.sum(expo, -1, keepdims=True)).astype(BF16)
        parts.append(jnp.dot(probs, values, preferred_element_type=F32).astype(BF16))
    attended = jnp.concatenate(parts, 1)
    width = kept_ref.shape[1]
    mine = pl.multiple_of(side * width, width)
    other = pl.multiple_of((1 - side) * width, width)
    handed_ref[...] = lax.dot_general(
        attended, w_ref[pl.ds(other, width), columns:], NT, preferred_element_type=F32
    ).astype(BF16)
    kept_ref[...] = lax.dot_general(
        attended, w_ref[pl.ds(mine, width), columns:], NT, preferred_element_type=F32
    )
    direct_ref[...] = lax.dot_general(
        attended, w_ref[2 * width :, columns:], NT, preferred_element_type=F32
    )


def combine_body(
    map_ref, shared_ref, both_ref, kept_ref, got_ref, direct_ref, own_ref, out_ref, own_out_ref
):
    width = kept_ref.shape[1]
    shared = jnp.dot(map_ref[...], shared_ref[...], preferred_element_type=F32)
    out_ref[:, :width] = (shared + kept_ref[...] + got_ref[...].astype(F32)).astype(BF16)
    both = jnp.dot(map_ref[...], both_ref[...], preferred_element_type=F32)
    out_ref[:, width:] = (both + direct_ref[...]).astype(BF16)


def local(
    residual_in,
    shortcut,
    attn_gain,
    moe_gain,
    query_weight,
    key_value,
    output_weight,
    query_gain,
    key_gain,
    router_weight,
    expert_ids,
    gate_up_weight,
    down_weight,
):
    n_ep = lax.axis_size("ep")
    n_tp = lax.axis_size("tp")
    rank = lax.axis_index("tp")
    rows, d_model = residual_in.shape
    direct_in = d_model // 8
    shared_in = (d_model - direct_in) // 2
    direct = d_model // 4
    shared = (d_model - direct) // 2
    places = n_ep * SLOTS
    ff2 = gate_up_weight.shape[2]
    ff = ff2 // 2
    qh_dev = query_weight.shape[1] // HD
    kv_head = rank * qh_dev // (QH // KVH)
    along_z = [[x * 16 + z * 2 + c for z in range(8)] for x in range(2) for c in range(2)]
    partner = [(i, i ^ 1) for i in range(n_tp)]

    own_key = lax.dynamic_slice_in_dim(key_value, kv_head * HD, HD, 1)
    own_value = lax.dynamic_slice_in_dim(key_value, (KVH + kv_head) * HD, HD, 1)
    packed = jnp.concatenate([query_weight, own_key, own_value, output_weight], 1)
    near = lax.all_gather(packed, "ep", axis=0, tiled=True, axis_index_groups=along_z)

    def to_owners(value):
        return lax.all_to_all(value, "ep", split_axis=0, concat_axis=0, tiled=True)

    def swapped(value):
        return lax.ppermute(value, "tp", partner)

    moe_gain = moe_gain[None, :]
    ids = expert_ids.T
    outgoing, outgoing_both = call(
        dispatch_body,
        [
            jax.ShapeDtypeStruct((places, shared_in), BF16),
            jax.ShapeDtypeStruct((places, direct_in), BF16),
        ],
        (shortcut, moe_gain, ids),
        2 * places * rows * (shared_in + direct_in),
    )
    arrived = to_owners(outgoing)
    received = swapped(arrived)
    arrived_both = to_owners(outgoing_both)
    (combine,) = call(
        combine_map_body,
        [jax.ShapeDtypeStruct((rows, places), BF16)],
        (shortcut, moe_gain, router_weight, ids),
        2 * rows * 128 * d_model,
        cost=0,
    )
    (acc,) = call(
        first_part_body,
        [jax.ShapeDtypeStruct((places, ff2), BF16)],
        (arrived, gate_up_weight),
        2 * places * shared_in * ff2,
        specs=[vmem(), anywhere()],
        scratch=[pltpu.VMEM((shared_in, ff2), BF16), pltpu.SemaphoreType.DMA],
    )
    out_both, handed, hidden = call(
        expert_body,
        [
            jax.ShapeDtypeStruct((places, direct), BF16),
            jax.ShapeDtypeStruct((places, shared), BF16),
            jax.ShapeDtypeStruct((places, ff), BF16),
        ],
        (acc, received, arrived_both, gate_up_weight, down_weight, near),
        2 * places * (shared_in + direct_in) * ff2 + 2 * places * ff * d_model,
        limit=52,
        specs=[anywhere(), vmem(), vmem()] + [anywhere()] * 3,
        out_specs=[anywhere()] * 3,
        scratch=[
            pltpu.VMEM((places, ff2), BF16),
            pltpu.VMEM((shared_in + direct_in, ff2), BF16),
            pltpu.VMEM((ff, shared + direct), BF16),
            pltpu.VMEM((places, ff), BF16),
            pltpu.VMEM((places, direct), BF16),
            pltpu.VMEM((places, shared), BF16),
            pltpu.SemaphoreType.DMA((32,)),
        ],
    )
    (kept,) = call(
        kept_body,
        [jax.ShapeDtypeStruct((places, shared), BF16)],
        (hidden, down_weight),
        0,
        cost=0,
        specs=[vmem(), anywhere()],
        scratch=[pltpu.VMEM((ff, shared), BF16), pltpu.SemaphoreType.DMA],
    )
    across = lax.ppermute(near, "ep", [(i, i ^ 16) for i in range(n_ep)])
    cores = [(i, i ^ 1) for i in range(n_ep)]
    other_near = lax.ppermute(near, "ep", cores)
    got = swapped(handed)
    returned_both = to_owners(out_both)
    expert_out = (kept.astype(F32) + got.astype(F32)).astype(BF16)
    returned = to_owners(expert_out)
    (across,) = call(
        relay_body,
        [jax.ShapeDtypeStruct(across.shape, BF16)],
        (across, expert_out),
        0,
        cost=0,
        limit=1,
        specs=[anywhere()] * 2,
        out_specs=[anywhere()],
        aliases={0: 0},
    )
    other_across = lax.ppermute(across, "ep", cores)

    position = jnp.arange(rows, dtype=F32)
    freq = ROPE_BASE ** (-jnp.arange(HD // 2, dtype=F32) * 2.0 / HD)
    angle = position[:, None] * freq[None, :]
    cosine, sine = jnp.cos(angle), jnp.sin(angle)
    cosine = jnp.concatenate([cosine, cosine], 1)
    sine = jnp.concatenate([-sine, sine], 1)
    att_handed, att_kept, att_both = call(
        attention_body,
        [
            jax.ShapeDtypeStruct((rows, shared), BF16),
            jax.ShapeDtypeStruct((rows, shared), F32),
            jax.ShapeDtypeStruct((rows, direct), F32),
        ],
        (
            residual_in,
            attn_gain[None, :],
            near,
            across,
            other_near,
            other_across,
            query_gain[None, :],
            key_gain[None, :],
            cosine,
            sine,
        ),
        2 * rows * d_model * packed.shape[1],
        cost=0,
        scratch=[pltpu.VMEM((d_model, packed.shape[1]), BF16)],
    )
    att_got = swapped(att_handed)
    share = rows // n_tp
    own = lax.dynamic_slice_in_dim(residual_in, rank * share, share, 0)
    total, own = call(
        combine_body,
        [
            jax.ShapeDtypeStruct((rows, shared + direct), BF16),
            jax.ShapeDtypeStruct(own.shape, BF16),
        ],
        (combine, returned, returned_both, att_kept, att_got, att_both, own),
        2 * rows * places * (shared + direct),
        limit=16,
        specs=[vmem()] * 6 + [anywhere()],
        out_specs=[vmem(), anywhere()],
        aliases={6: 1},
    )
    terms = lax.all_to_all(
        total.reshape(n_tp, share, shared + direct),
        "tp",
        split_axis=0,
        concat_axis=0,
        tiled=True,
    )
    terms = terms.astype(F32)
    sums = [jnp.sum(terms[h::2, :, :shared], 0) for h in range(2)]
    sums = jnp.concatenate(sums + [jnp.sum(terms[:, :, shared:], 0)], 1)
    mine = (own.astype(F32) + sums).astype(BF16)
    everyone = lax.all_to_all(
        jnp.broadcast_to(mine[None], (n_tp, share, d_model)),
        "tp",
        split_axis=0,
        concat_axis=0,
        tiled=True,
    )
    return everyone.reshape(rows, d_model)


def solution(mesh):
    return jax.shard_map(
        local,
        mesh=mesh,
        in_specs=(
            P("ep", None),
            P("ep", None),
            P(),
            P(),
            P("ep", "tp"),
            P("ep", None),
            P("ep", "tp"),
            P(),
            P(),
            P(),
            P("ep", None),
            P(("ep", "tp"), None, None),
            P(("ep", "tp"), None, None),
        ),
        out_specs=P("ep", None),
        check_vma=False,
    )
```
